256 devices in a mesh: section: 8 (over x_lo, y), dp: 32 (over x_hi, z, core).
Axes of the slice: x: 4 (x_hi: 2, x_lo: 2; x = x_hi * 2 + x_lo), y: 4, z: 8, core: 2. Of those that a mesh axis runs over, the one named last changes fastest.
Arguments:
- stashed: bfloat16 [8, 4096, 2048], P('section', 'dp'), as said below
- grad_top: bfloat16 [4096, 2048], P('dp'), may hold values from -6 to 6
- lengths: int32 [128], P('dp'), may hold values from 1 to 32, as said below
- norm_gain: bfloat16 [8, 2048], P('section', 'dp'), may hold values from 0.099609375 to 1.8984375
- qkv_weight: bfloat16 [8, 2048, 1280], P('section', 'dp'), may hold values from -0.125 to 0.125
- out_weight: bfloat16 [8, 1024, 2048], P('section', 'dp'), may hold values from -0.1875 to 0.1875
Outputs:
- stashed_grad: bfloat16 [8, 4096, 2048], P('section', 'dp')
- gain_grad: float32 [8, 2048], P('section', 'dp')
- qkv_grad: float32 [8, 2048, 1280], P('section', 'dp')
- out_grad: float32 [8, 1024, 2048], P('section', 'dp')
The draws below stay inside these ranges and needn't reach their ends.
Inputs may be any that keep to these rules, and one draw needn't show every extreme that they name: `lengths`: positions at or past a sequence's length are padding that no query attends to. `stashed`: activations of varied scale across tokens and features.
All inputs are finite; a program needn't handle non-finite values.
Results may differ from the reference program's by a relative error of at most 0.035.
Values may be sent and summed in bfloat16 or wider, within the bound.
No kernel may reach another device: no remote copies, remote signals or barrier semaphores. Data moves between devices by JAX's collectives and lax.ppermute only.
A program may use at most 128 MiB of HBM per device.

```python
import math
import jax
import jax.numpy as jnp
from jax import lax

D = 2048
HD = 64
H = 16
KVH = 2
SEQLEN = 32
SECTIONS = 8
QW = 1024
QKVW = 1280
TOK_DEV = 128
TOKENS = 4096
SEQS = 128
N_DP = 32


def draw_stashed(key, part):
    key = jax.random.fold_in(key, 5)
    noise_key, row_key, col_key = jax.random.split(key, 3)
    shape_all = (SECTIONS, TOKENS, D)
    noise_values = jnp.clip(jax.random.normal(noise_key, shape_all, jnp.float32), -4.0, 4.0)
    row_scale = jnp.exp(jax.random.uniform(row_key, (SECTIONS, TOKENS, 1), jnp.float32) * math.log(10.0))
    col_scale = jnp.exp(jax.random.uniform(col_key, (SECTIONS, 1, D), jnp.float32) * math.log(10.0))
    return (noise_values * row_scale * col_scale).astype(jnp.bfloat16)


def draw_lengths(key, part):
    key = jax.random.fold_in(key, 9)
    history = jax.random.randint(key, (SEQS,), 1, 2 * SEQLEN, dtype=jnp.int32)
    history = jnp.minimum(history, SEQLEN)
    return history.at[0].set(SEQLEN).astype(jnp.int32)


def shard_levels(stream_key, dims, shards, smallest, high):
    level, own = 1.0, jax.random.fold_in(stream_key, 6)
    for position, shards_of in shards:
        heights = jnp.exp(jax.random.uniform(jax.random.fold_in(own, position), (shards_of,), jnp.float32, smallest / len(shards), high / len(shards)))
        level = level * jnp.repeat(heights, dims[position] // shards_of).reshape([-1 if axis == position else 1 for axis in range(len(dims))])
    return level


def noise(key, dims, width, limit, cuts=(), kind=jnp.bfloat16):
    entries = jax.random.normal(key, dims, jnp.float32) * width
    if len(cuts) > 0:
        entries = shard_levels(key, dims, cuts, -0.22, 0.18) * entries
    return jnp.clip(entries, min=-limit, max=limit).astype(kind)


def setup_inputs(seed: int = 0) -> dict:
    keys = jax.random.split(jax.random.key(seed), 7)
    stashed = draw_stashed(jax.random.fold_in(keys[6], 71), 0)
    grad_top = noise(keys[1], (TOKENS, D), 1.0, 6.0, ((0, 32),))
    lengths = draw_lengths(jax.random.fold_in(keys[6], 71), 0)
    norm_gain = jnp.clip(1.0 + 0.18 * jax.random.normal(keys[3], (SECTIONS, D), jnp.float32), 0.099609375, 1.8984375).astype(jnp.bfloat16)
    qkv_weight = noise(keys[4], (SECTIONS, D, QKVW), D ** -0.5, 0.125, ((0, 8), (1, 32)))
    out_weight = noise(keys[5], (SECTIONS, QW, D), QW ** -0.5, 0.1875, ((0, 8), (1, 32)))
    return {"stashed": stashed, "grad_top": grad_top, "lengths": lengths, "norm_gain": norm_gain, "qkv_weight": qkv_weight, "out_weight": out_weight}


EPSILON = 1e-05
ROPE_BASE = 10000.0

def rope_tables(seq_len, head_dim):
    half_dim = head_dim // 2
    inverse_freq = ROPE_BASE ** (-(jnp.arange(half_dim, dtype=jnp.float32) * 2.0 / head_dim))
    angles = jnp.arange(seq_len, dtype=jnp.float32)[:, None] * inverse_freq[None, :]
    return (jnp.cos(angles)[None, :, None, :], jnp.sin(angles)[None, :, None, :])

def rotate_pairs(values, cosine, sine):
    half_dim = values.shape[-1] // 2
    first_half = values[..., :half_dim]
    second_half = values[..., half_dim:]
    return jnp.concatenate([first_half * cosine - second_half * sine, second_half * cosine + first_half * sine], axis=-1)

def layer_backward(inputs, cotangent, seq_lengths, gain_row, qkv_matrix, out_matrix, heads, kv_heads, head_dim, seq_len):
    rows_count = inputs.shape[0]
    seq_count = rows_count // seq_len
    query_width = heads * head_dim
    kv_width = kv_heads * head_dim
    group_size = heads // kv_heads
    scale_factor = head_dim ** (-0.5)
    cosine, sine = rope_tables(seq_len, head_dim)
    wide_inputs = inputs.astype(jnp.float32)
    inverse_rms = lax.rsqrt(lax.optimization_barrier(jnp.mean(wide_inputs * wide_inputs, axis=1, keepdims=True)) + EPSILON)
    gain_wide = gain_row.astype(jnp.float32)[None, :]
    normed = (wide_inputs * inverse_rms * gain_wide).astype(jnp.bfloat16)
    projected = jnp.dot(normed, qkv_matrix, preferred_element_type=jnp.float32)
    queries = projected[:, :query_width].reshape(seq_count, seq_len, heads, head_dim)
    key_rows = projected[:, query_width:query_width + kv_width].reshape(seq_count, seq_len, kv_heads, head_dim)
    value_rows = projected[:, query_width + kv_width:].reshape(seq_count, seq_len, kv_heads, head_dim)
    queries = rotate_pairs(queries, cosine, sine).astype(jnp.bfloat16)
    key_rows = rotate_pairs(key_rows, cosine, sine).astype(jnp.bfloat16)
    value_rows = value_rows.astype(jnp.bfloat16)
    grouped = queries.reshape(seq_count, seq_len, kv_heads, group_size, head_dim)
    scores = jnp.einsum('sikgd,sjkd->skgij', grouped.astype(jnp.float32), key_rows.astype(jnp.float32)) * scale_factor
    positions = jnp.arange(seq_len, dtype=jnp.int32)
    causal = positions[None, :] <= positions[:, None]
    present = positions[None, :] < seq_lengths.astype(jnp.int32)[:, None]
    allowed = jnp.logical_and(causal[None, None, None, :, :], present[:, None, None, None, :])
    exponent_terms = jnp.where(allowed, jnp.exp(jnp.where(allowed, scores, 0.0)), 0.0)
    probs = exponent_terms / lax.optimization_barrier(jnp.sum(exponent_terms, axis=-1, keepdims=True))
    probs_low = probs.astype(jnp.bfloat16)
    attended = jnp.einsum('skgij,sjkd->sikgd', probs_low.astype(jnp.float32), value_rows.astype(jnp.float32))
    attended = attended.reshape(rows_count, query_width).astype(jnp.bfloat16)
    grad_attended = lax.dot_general(cotangent, out_matrix, (((1,), (1,)), ((), ())), preferred_element_type=jnp.float32).astype(jnp.bfloat16)
    grad_grouped = grad_attended.reshape(seq_count, seq_len, kv_heads, group_size, head_dim).astype(jnp.float32)
    grad_probs = jnp.einsum('sikgd,sjkd->skgij', grad_grouped, value_rows.astype(jnp.float32))
    grad_values = jnp.einsum('skgij,sikgd->sjkd', probs_low.astype(jnp.float32), grad_grouped)
    grad_scores = (probs * (grad_probs - lax.optimization_barrier(jnp.sum(probs * grad_probs, axis=-1, keepdims=True))) * scale_factor).astype(jnp.bfloat16)
    grad_queries = jnp.einsum('skgij,sjkd->sikgd', grad_scores.astype(jnp.float32), key_rows.astype(jnp.float32))
    grad_queries = grad_queries.reshape(seq_count, seq_len, heads, head_dim)
    grad_keys = jnp.einsum('skgij,sikgd->sjkd', grad_scores.astype(jnp.float32), grouped.astype(jnp.float32))
    grad_queries = rotate_pairs(grad_queries, cosine, -sine)
    grad_keys = rotate_pairs(grad_keys, cosine, -sine)
    grad_projected = jnp.concatenate([grad_queries.reshape(rows_count, query_width), grad_keys.reshape(rows_count, kv_width), grad_values.reshape(rows_count, kv_width)], axis=1).astype(jnp.bfloat16)
    grad_normed = lax.dot_general(grad_projected, qkv_matrix, (((1,), (1,)), ((), ())), preferred_element_type=jnp.float32)
    gain_terms = grad_normed * wide_inputs * inverse_rms
    grad_hat = grad_normed * gain_wide
    grad_inner = inverse_rms * (grad_hat - wide_inputs * inverse_rms * inverse_rms * lax.optimization_barrier(jnp.mean(grad_hat * wide_inputs, axis=1, keepdims=True)))
    grad_inputs = (cotangent.astype(jnp.float32) + grad_inner).astype(jnp.bfloat16)
    return (grad_inputs, gain_terms, normed, grad_projected, attended)

def contract_rows(left, right):
    return lax.dot_general(left, right, (((0,), (0,)), ((), ())), preferred_element_type=jnp.float32)

def rounded(values):
    narrow = values.astype(jnp.bfloat16)
    narrow = lax.optimization_barrier(narrow)
    return narrow.astype(jnp.float32)

def add_shard(totals, pieces):
    normed, grad_projected, attended, cotangent, gain_terms = pieces
    part_gain = rounded(lax.optimization_barrier(jnp.sum(gain_terms, axis=0)))
    part_qkv = rounded(contract_rows(normed, grad_projected))
    part_out = rounded(contract_rows(attended, cotangent))
    return ((totals[0] + part_gain, totals[1] + part_qkv, totals[2] + part_out), None)

def reference(stashed, grad_top, lengths, norm_gain, qkv_weight, out_weight):
    cotangent = grad_top
    input_grads = [None] * SECTIONS
    gain_grads = [None] * SECTIONS
    qkv_grads = [None] * SECTIONS
    out_grads = [None] * SECTIONS
    for layer_id in range(SECTIONS - 1, -1, -1):
        grad_inputs, gain_terms, normed, grad_projected, attended = layer_backward(stashed[layer_id], cotangent, lengths, norm_gain[layer_id], qkv_weight[layer_id], out_weight[layer_id], H, KVH, HD, SEQLEN)
        shard_pieces = (normed.reshape(N_DP, TOK_DEV, D), grad_projected.reshape(N_DP, TOK_DEV, QKVW), attended.reshape(N_DP, TOK_DEV, QW), cotangent.reshape(N_DP, TOK_DEV, D), gain_terms.reshape(N_DP, TOK_DEV, D))
        zero_state = (jnp.zeros((D,), jnp.float32), jnp.zeros((D, QKVW), jnp.float32), jnp.zeros((QW, D), jnp.float32))
        totals, unused = lax.scan(add_shard, zero_state, shard_pieces)
        input_grads[layer_id] = grad_inputs
        gain_grads[layer_id] = totals[0]
        qkv_grads[layer_id] = totals[1]
        out_grads[layer_id] = totals[2]
        cotangent = grad_inputs
    return (jnp.stack(input_grads), jnp.stack(gain_grads), jnp.stack(qkv_grads), jnp.stack(out_grads))
```

```python
import jax
import jax.numpy as jnp
from jax import lax
from jax.experimental import pallas as pl
from jax.experimental.pallas import tpu as pltpu
from jax.sharding import PartitionSpec as P

D = 2048
HD = 64
SEQLEN = 32
QW = 1024
KVW = 128
QKVW = 1280
TOK = 128
MB = 2
NB = TOK // MB
LAYERS = 8
NZ = 8
NDP = 32
QUADS = 4
QL = 256
EPSILON = 1e-05
ROPE_BASE = 10000.0
BF = jnp.bfloat16
F32 = jnp.float32
VMEM_LIMIT = 40 << 20
PACKW = QKVW + 1024 + 128

ANY = pl.BlockSpec(memory_space=pl.ANY)
VM = pl.BlockSpec(memory_space=pltpu.VMEM)
SM = pl.BlockSpec(memory_space=pltpu.SMEM)


def nn(a, b):
    return lax.dot_general(a, b, (((1,), (0,)), ((), ())), preferred_element_type=F32)


def nt(a, b):
    return lax.dot_general(a, b, (((1,), (1,)), ((), ())), preferred_element_type=F32)


def tn(a, b):
    return lax.dot_general(a, b, (((0,), (0,)), ((), ())), preferred_element_type=F32)


def rotate(u, cosine, sine):
    rows = u.shape[0]
    lane = lax.broadcasted_iota(jnp.int32, (rows, 128), 1)
    first = (lane & 63) < 32
    parts = []
    for i in range(u.shape[1] // 128):
        block = u[:, i * 128 : (i + 1) * 128]
        swapped = jnp.where(first, pltpu.roll(block, 96, 1), pltpu.roll(block, 32, 1))
        parts.append(block * cosine + swapped * sine)
    return parts[0] if len(parts) == 1 else jnp.concatenate(parts, axis=1)


def half_sums(values):
    rows = values.shape[0]
    lane = lax.broadcasted_iota(jnp.int32, (rows, 128), 1)
    low = lane < 64
    parts = []
    for i in range(values.shape[1] // 128):
        block = values[:, i * 128 : (i + 1) * 128]
        left = jnp.sum(jnp.where(low, block, 0.0), axis=1, keepdims=True)
        right = jnp.sum(jnp.where(low, 0.0, block), axis=1, keepdims=True)
        parts.append(jnp.where(low, left, right))
    return jnp.concatenate(parts, axis=1)


def block_diagonal_mask():
    row = lax.broadcasted_iota(jnp.int32, (QL, QL), 0)
    lane = lax.broadcasted_iota(jnp.int32, (QL, QL), 1)
    return (row >> 6) == (lane >> 6)


def block_diagonal(rows128, group, mask):
    lane = lax.broadcasted_iota(jnp.int32, rows128.shape, 1)
    other = pltpu.roll(rows128, 64, 1)
    keep = (lane < 64) if group == 0 else (lane >= 64)
    twice = jnp.where(keep, rows128, other)
    wide = jnp.concatenate([twice, twice], axis=1)
    tall = jnp.concatenate([wide] * 4, axis=0)
    return jnp.where(mask, tall, 0.0).astype(BF)


def fold_diagonal(products, mask):
    kept = jnp.where(mask, products, 0.0)
    tall = kept[0:64] + kept[64:128] + kept[128:192] + kept[192:256]
    pair = tall[:, :128] + tall[:, 128:]
    return pair + pltpu.roll(pair, 64, 1)


def forward_kernel(place, lengths, x_ref, cos_ref, sin_ref, *refs):
    pieces = refs[:32]
    (wq_ref, wo_ref, gain_ref, scale_ref, probs_ref, q_ref, bdk_ref, bdv_ref,
     normed_ref, attended_ref, gain_pieces, sems) = refs[32:]
    copies_q = []
    copies_o = []
    for i, piece in enumerate(pieces):
        owner = place[i]
        row64 = pl.multiple_of(owner * 64, 64)
        row32 = pl.multiple_of(owner * 32, 32)
        row16 = pl.multiple_of(owner * 16, 16)
        copies_q.append(pltpu.make_async_copy(
            piece.at[0:16, pl.ds(QKVW + 1024, 128)], gain_pieces.at[pl.ds(row16, 16), :], sems.at[4 * i]))
        copies_q.append(pltpu.make_async_copy(
            piece.at[:, pl.ds(0, QKVW)], wq_ref.at[pl.ds(row64, 64), :], sems.at[4 * i + 1]))
        for j in range(2):
            copies_o.append(pltpu.make_async_copy(
                piece.at[pl.ds(32 * j, 32), pl.ds(QKVW, 1024)],
                wo_ref.at[pl.ds(row32, 32), pl.ds(1024 * j, 1024)], sems.at[4 * i + 2 + j]))
    for copy in copies_q:
        copy.start()
    for copy in copies_o:
        copy.start()
    wide = x_ref[...].astype(F32)
    inverse = lax.rsqrt(jnp.sum(wide * wide, axis=1, keepdims=True) * (1.0 / D) + EPSILON)
    scale_ref[...] = jnp.broadcast_to(inverse, (TOK, 128))
    mask = block_diagonal_mask()
    for copy in copies_q:
        copy.wait()
    for i in range(16):
        both = (gain_pieces[pl.ds(32 * i, 1), :].astype(F32)
                + gain_pieces[pl.ds(32 * i + 16, 1), :].astype(F32))
        gain_ref[:, pl.ds(128 * i, 128)] = jnp.broadcast_to(both, (8, 128))
    normed = (wide * inverse * gain_ref[0:1, :]).astype(BF)
    for i in range(16):
        normed_ref[i] = normed[:, i * 128 : (i + 1) * 128]
    projected = nn(normed, wq_ref[...])
    cosine = cos_ref[...]
    sine = sin_ref[...]
    queries = rotate(projected[:, :QW], cosine, sine).astype(BF)
    keys = rotate(projected[:, QW : QW + KVW], cosine, sine).astype(BF).astype(F32)
    values = projected[:, QW + KVW :].astype(BF).astype(F32)
    row = lax.broadcasted_iota(jnp.int32, (NB, QL), 0)
    lane = lax.broadcasted_iota(jnp.int32, (NB, QL), 1) & 63
    for m in range(MB):
        rows = slice(m * NB, (m + 1) * NB)
        length = jnp.where(row < SEQLEN, lengths[2 * m], lengths[2 * m + 1])
        allowed = ((row >> 5) == (lane >> 5)) & (lane <= row) & ((lane & 31) < length)
        for g in range(2):
            bdk = block_diagonal(keys[rows], g, mask)
            bdv = block_diagonal(values[rows], g, mask)
            bdk_ref[m, g] = bdk
            bdv_ref[m, g] = bdv
            for t in (2 * g, 2 * g + 1):
                quad = queries[rows, t * QL : (t + 1) * QL]
                q_ref[m, pl.ds(t * NB, NB), :] = quad
                scores = nt(quad, bdk) * 0.125
                terms = jnp.where(allowed, jnp.exp(jnp.where(allowed, scores, 0.0)), 0.0)
                probs = terms / half_sums(terms)
                probs_ref[m, pl.ds(t * NB, NB), :] = probs
                got = nn(probs.astype(BF), bdv).astype(BF)
                attended_ref[t // 2, pl.ds(m * NB, NB), pl.ds((t % 2) * QL, QL)] = got
    for copy in copies_o:
        copy.wait()


def forward(place, lengths, inputs, cosine, sine, pieces):
    shapes = [
        ((D, QKVW), BF), ((QW, D), BF), ((8, D), F32), ((TOK, 128), F32),
        ((MB, QUADS * NB, QL), F32), ((MB, QUADS * NB, QL), BF),
        ((MB, 2, QL, QL), BF), ((MB, 2, QL, QL), BF),
        ((16, TOK, 128), BF), ((2, TOK, 512), BF),
    ]
    return pl.pallas_call(
        forward_kernel,
        out_shape=[jax.ShapeDtypeStruct(s, t) for s, t in shapes],
        in_specs=[SM, SM, VM, VM, VM] + [ANY] * 32,
        out_specs=[VM] * len(shapes),
        scratch_shapes=[pltpu.VMEM((NDP * 16, 128), BF), pltpu.SemaphoreType.DMA((128,))],
        compiler_params=pltpu.CompilerParams(vmem_limit_bytes=VMEM_LIMIT),
        name="forward",
    )(place, lengths, inputs, cosine, sine, *pieces)


def tick_kernel(plan, cot_ref, top_ref, x_ref, gain_ref, scale_ref, wq_ref, wo_ref, probs_ref, q_ref,
                bdk_ref, bdv_ref, cos_ref, sin_ref, out_ref, gp_ref):
    @pl.when(plan[0] == 1)
    def _():
        m = plan[1]
        first = pl.multiple_of(m * NB, NB)
        cot = jnp.where(plan[2] == 1, top_ref[pl.ds(first, NB), :], cot_ref[...])
        grad_att = nt(cot, wo_ref[...]).astype(BF)
        mask = block_diagonal_mask()
        cosine = cos_ref[pl.ds(0, NB), :]
        sine = -sin_ref[pl.ds(0, NB), :]
        parts = []
        grad_keys = []
        grad_values = []
        for g in range(2):
            bdk = bdk_ref[m, g]
            bdv = bdv_ref[m, g]
            rows = pl.ds(g * 2 * NB, 2 * NB)
            quads = jnp.concatenate(
                [grad_att[:, (2 * g + i) * QL : (2 * g + i + 1) * QL] for i in range(2)], axis=0)
            probs = probs_ref[m, rows, :]
            grad_probs = nt(quads, bdv)
            centre = half_sums(probs * grad_probs)
            grad_scores = (probs * (grad_probs - centre) * 0.125).astype(BF)
            grad_q = nn(grad_scores, bdk)
            parts.append(grad_q[:NB])
            parts.append(grad_q[NB:])
            grad_keys.append(fold_diagonal(tn(grad_scores, q_ref[m, rows, :]), mask))
            grad_values.append(fold_diagonal(tn(probs.astype(BF), quads), mask))
        lane = lax.broadcasted_iota(jnp.int32, (NB, 128), 1)
        key_rows = jnp.where(lane < 64, grad_keys[0], grad_keys[1])
        value_rows = jnp.where(lane < 64, grad_values[0], grad_values[1])
        rotated = rotate(jnp.concatenate(parts + [key_rows], axis=1), cosine, sine)
        gp = jnp.concatenate([rotated, value_rows], axis=1).astype(BF)
        gp_ref[...] = gp
        grad_hat = nt(gp, wq_ref[...]) * gain_ref[0:1, :]
        wide = x_ref[pl.ds(first, NB), :].astype(F32)
        inverse = scale_ref[pl.ds(first, NB), :][:, 0:1]
        mean = jnp.sum(grad_hat * wide, axis=1, keepdims=True) * (1.0 / D)
        inner = inverse * (grad_hat - wide * (inverse * inverse * mean))
        out_ref[...] = (cot.astype(F32) + inner).astype(BF)


def tick(plan, cot, top, inputs, gain, scale, wq, wo, probs, q, bdk, bdv, cosine, sine):
    return pl.pallas_call(
        tick_kernel,
        out_shape=[jax.ShapeDtypeStruct((NB, D), BF), jax.ShapeDtypeStruct((NB, QKVW), BF)],
        in_specs=[SM] + [VM] * 13,
        out_specs=[VM, VM],
        compiler_params=pltpu.CompilerParams(vmem_limit_bytes=VMEM_LIMIT),
        name="tick",
    )(plan, cot, top, inputs, gain, scale, wq, wo, probs, q, bdk, bdv, cosine, sine)


def choose_kernel(groups, which, *refs):
    total = sum(groups)
    outs = refs[total : total + len(groups)]
    sem = refs[-1]
    base = 0
    for i, count in enumerate(groups):
        for j in range(count):
            @pl.when(which[i] == j)
            def _(source=refs[base + j], target=outs[i], i=i):
                pltpu.make_async_copy(source, target, sem.at[i]).start()
        base += count
    base = 0
    for i, count in enumerate(groups):
        pltpu.make_async_copy(refs[base], outs[i], sem.at[i]).wait()
        base += count


def choose(which, candidates, name):
    groups = [len(c) for c in candidates]
    flat = [a for c in candidates for a in c]
    return pl.pallas_call(
        lambda *refs: choose_kernel(groups, *refs),
        out_shape=[jax.ShapeDtypeStruct(c[0].shape, c[0].dtype) for c in candidates],
        in_specs=[SM] + [ANY] * len(flat),
        out_specs=[ANY] * len(groups),
        scratch_shapes=[pltpu.SemaphoreType.DMA((len(groups),))],
        name=name,
    )(which, *flat)


def qkv_terms_kernel(place, *refs):
    normed = refs[:4]
    gp = refs[4:8]
    outs = refs[8:]
    right = jnp.concatenate([r[...] for r in gp], axis=0)
    for k in range(NZ):
        chunk = (place[0] + k) & 7
        left = jnp.concatenate([r[chunk] for r in normed], axis=0)
        outs[k][...] = tn(left, right).astype(BF)


def out_terms_kernel(place, *refs):
    attended = refs[:4]
    cot = refs[4:8]
    outs = refs[8:16]
    scratch = refs[16]
    left = jnp.concatenate([r[...] for r in attended], axis=0)
    right = jnp.concatenate([r[...] for r in cot], axis=0)
    total = tn(left, right).astype(BF)
    for z in range(NZ):
        scratch[z] = total[z * 64 : (z + 1) * 64]
    for k in range(NZ):
        outs[k][...] = scratch[(place[0] + k) & 7]


def qkv_terms(place, normed, gp):
    return pl.pallas_call(
        qkv_terms_kernel,
        out_shape=[jax.ShapeDtypeStruct((128, 640), BF)] * NZ,
        in_specs=[SM] + [VM] * 8,
        out_specs=[VM] * NZ,
        compiler_params=pltpu.CompilerParams(vmem_limit_bytes=VMEM_LIMIT),
        name="qkv_terms",
    )(place, *normed, *gp)


def out_terms(place, attended, cot):
    return pl.pallas_call(
        out_terms_kernel,
        out_shape=[jax.ShapeDtypeStruct((64, 1024), BF)] * NZ,
        in_specs=[SM] + [VM] * 8,
        out_specs=[VM] * NZ,
        scratch_shapes=[pltpu.VMEM((NZ, 64, 1024), BF)],
        compiler_params=pltpu.CompilerParams(vmem_limit_bytes=VMEM_LIMIT),
        name="out_terms",
    )(place, *attended, *cot)


def add_kernel(*refs):
    out = refs[-1]
    total = refs[0][...].astype(F32)
    for r in refs[1:-1]:
        total = total + r[...].astype(F32)
    half = total.shape[0] // 2
    out[0] = total[:half]
    out[1] = total[half:]


def add_terms(parts):
    rows, width = parts[0].shape
    return pl.pallas_call(
        add_kernel,
        out_shape=jax.ShapeDtypeStruct((2, rows // 2, width), F32),
        in_specs=[VM] * len(parts),
        out_specs=VM,
        compiler_params=pltpu.CompilerParams(vmem_limit_bytes=VMEM_LIMIT),
        name="add_terms",
    )(*parts)


def dp_index(x, z, c):
    return (x * NZ + z) * 2 + c


def along_z(value, steps):
    return lax.ppermute(value, "dp", [
        (dp_index(x, z, c), dp_index(x, (z + steps) % NZ, c))
        for x in range(2) for z in range(NZ) for c in range(2)])


def across_x(value):
    return lax.ppermute(value, "dp", [(i, i ^ 16) for i in range(NDP)])


def across_core(value):
    return lax.ppermute(value, "dp", [(i, i ^ 1) for i in range(NDP)])


def pick(pair, index):
    return lax.dynamic_index_in_dim(pair, index, 0, keepdims=False)


def body(stashed, grad_top, lengths, norm_gain, qkv_weight, out_weight):
    section = lax.axis_index("section")
    dp = lax.axis_index("dp")
    x_place = dp // 16
    z_place = (dp // 2) % NZ
    core = dp % 2
    inputs = stashed[0]

    gain = norm_gain.reshape(1, 64)
    zero = jnp.zeros_like(gain)
    gain_pair = jnp.where(core == 0, jnp.concatenate([gain, zero], 1), jnp.concatenate([zero, gain], 1))
    packed = jnp.concatenate([
        qkv_weight[0],
        jnp.concatenate([out_weight[0][:, :1024], out_weight[0][:, 1024:]], axis=0),
        jnp.broadcast_to(gain_pair, (64, 128)),
    ], axis=1)
    own = [packed, across_x(packed)]
    pieces = [(own[0], 0, 0), (own[1], 1, 0)]
    up, down = list(own), list(own)
    for k in range(1, 4):
        up = [along_z(v, 1) for v in up]
        down = [along_z(v, -1) for v in down]
        for s in range(2):
            pieces.append((up[s], s, -k))
            pieces.append((down[s], s, k))
    pieces.append((along_z(up[0], 1), 0, 4))
    pieces.append((along_z(down[1], -1), 1, 4))
    arrays = [p[0] for p in pieces] + [across_core(p[0]) for p in pieces]
    place = jnp.stack(
        [dp_index(x_place ^ s, (z_place + dz) % NZ, core ^ c) for c in range(2) for _, s, dz in pieces]
    ).astype(jnp.int32)

    half = HD // 2
    inverse_freq = ROPE_BASE ** (-(jnp.arange(half, dtype=F32) * 2.0 / HD))
    angles = jnp.arange(SEQLEN, dtype=F32)[:, None] * inverse_freq[None, :]
    cosine = jnp.tile(jnp.cos(angles), (TOK // SEQLEN, 4))
    sine = jnp.sin(angles)
    sine = jnp.tile(jnp.concatenate([-sine, sine], axis=1), (TOK // SEQLEN, 2))

    (wq, wo, gain_row, scale, probs, q, bdk, bdv, normed, attended) = forward(
        place, lengths, inputs, cosine, sine, arrays)

    def gathered(halves):
        mine = pick(halves, x_place)
        other = across_x(pick(halves, 1 - x_place))
        return [mine, other, across_core(mine), across_core(other)]

    normed_blocks = gathered(normed.reshape(2, NZ, TOK, 128))
    attended_blocks = gathered(attended)

    ticks = LAYERS + MB - 1
    incoming = jnp.zeros((NB, D), BF)
    arrived, sent, projected_grads = [], [], []
    for t in range(ticks):
        micro = t - (LAYERS - 1) + section
        active = jnp.logical_and(micro >= 0, micro < MB)
        plan = jnp.stack([active, jnp.clip(micro, 0, MB - 1), section == LAYERS - 1]).astype(jnp.int32)
        arrived.append(incoming)
        out, gp = tick(plan, incoming, grad_top, inputs, gain_row, scale, wq, wo, probs, q, bdk, bdv,
                       cosine, sine)
        sent.append(out)
        projected_grads.append(gp)
        if t + 1 < ticks:
            pairs = [(s, s - 1) for s in range(1, LAYERS) if 0 <= t - (LAYERS - 1) + s < MB]
            incoming = lax.ppermute(out, "section", pairs)

    first_tick = (LAYERS - 1) - section
    is_top = section == LAYERS - 1
    which = jnp.stack([first_tick] * 6).astype(jnp.int32)
    cots, gps, gis = [], [], []
    for m in range(MB):
        cand = [grad_top[m * NB : (m + 1) * NB]] + [arrived[t + m] for t in range(1, LAYERS)]
        cot, gp, gi = choose(which, [cand, projected_grads[m : m + LAYERS], sent[m : m + LAYERS]], "choose")
        cots.append(cot)
        gps.append(gp)
        gis.append(gi)
    cot = jnp.concatenate(cots, axis=0)
    gp = jnp.concatenate(gps, axis=0)
    grads_in = jnp.concatenate(gis, axis=0)

    def column_blocks(value):
        width = value.shape[1] // 2
        both = [value, across_x(value)]
        mine = [jnp.where(core == 0, v[:, :width], v[:, width:]) for v in both]
        other = [jnp.where(core == 0, v[:, width:], v[:, :width]) for v in both]
        return mine + [across_core(v) for v in other]

    z_index = z_place.reshape(1).astype(jnp.int32)

    def summed(chunks):
        got = [chunks[0]] + [along_z(chunks[k], k) for k in range(1, NZ)]
        total = add_terms(got)
        kept = pick(total, core)
        other = across_core(pick(total, 1 - core))
        return jnp.where(core == 0, jnp.concatenate([kept, other], 1), jnp.concatenate([other, kept], 1))

    out_grad = summed(out_terms(z_index, attended_blocks, column_blocks(cot)))
    qkv_grad = summed(qkv_terms(z_index, normed_blocks, column_blocks(gp)))
    gain_grad = jnp.sum(qkv_grad * qkv_weight[0].astype(F32), axis=1) / norm_gain[0].astype(F32)
    return (grads_in[None], gain_grad[None], qkv_grad[None], out_grad[None])


def solution(mesh):
    in_specs = (
        P("section", "dp", None),
        P("dp", None),
        P("dp"),
        P("section", "dp"),
        P("section", "dp", None),
        P("section", "dp", None),
    )
    out_specs = (
        P("section", "dp", None),
        P("section", "dp"),
        P("section", "dp", None),
        P("section", "dp", None),
    )
    return jax.shard_map(body, mesh=mesh, in_specs=in_specs, out_specs=out_specs, check_vma=False)
```

```python
from functools import partial

import jax
import jax.numpy as jnp
import numpy as np
from jax import lax
from jax.experimental import pallas as pl
from jax.experimental.pallas import tpu as pltpu
from jax.sharding import PartitionSpec as P

D = 2048
HD = 64
SEQLEN = 32
QW = 1024
KVW = 128
QKVW = 1280
TOK = 128
MB = 2
NB = TOK // MB
LAYERS = 8
NZ = 8
NDP = 32
QUADS = 4
QL = 256
EPSILON = 1e-05
ROPE_BASE = 10000.0
BF = jnp.bfloat16
F32 = jnp.float32
VMEM_LIMIT = 28 << 20
SMALL_LIMIT = 12 << 20
SEC, XP, ZP, CORE = range(4)
PACKW = QKVW + 1024 + 128

ANY = pl.BlockSpec(memory_space=pl.ANY)
VM = pl.BlockSpec(memory_space=pltpu.VMEM)
SM = pl.BlockSpec(memory_space=pltpu.SMEM)


def held(value):
    return pltpu.with_memory_space_constraint(value, pltpu.VMEM)


def nn(a, b):
    return lax.dot_general(a, b, (((1,), (0,)), ((), ())), preferred_element_type=F32)


def nt(a, b):
    return lax.dot_general(a, b, (((1,), (1,)), ((), ())), preferred_element_type=F32)


def tn(a, b):
    return lax.dot_general(a, b, (((0,), (0,)), ((), ())), preferred_element_type=F32)


def rotate(u, cosine, sine):
    rows = u.shape[0]
    lane = lax.broadcasted_iota(jnp.int32, (rows, 128), 1)
    first = (lane & 63) < 32
    parts = []
    for i in range(u.shape[1] // 128):
        block = u[:, i * 128 : (i + 1) * 128]
        swapped = jnp.where(first, pltpu.roll(block, 96, 1), pltpu.roll(block, 32, 1))
        parts.append(block * cosine + swapped * sine)
    return parts[0] if len(parts) == 1 else jnp.concatenate(parts, axis=1)


def half_sums(values):
    rows = values.shape[0]
    lane = lax.broadcasted_iota(jnp.int32, (rows, 128), 1)
    low = lane < 64
    parts = []
    for i in range(values.shape[1] // 128):
        block = values[:, i * 128 : (i + 1) * 128]
        left = jnp.sum(jnp.where(low, block, 0.0), axis=1, keepdims=True)
        right = jnp.sum(jnp.where(low, 0.0, block), axis=1, keepdims=True)
        parts.append(jnp.where(low, left, right))
    return jnp.concatenate(parts, axis=1)


def block_diagonal_mask():
    row = lax.broadcasted_iota(jnp.int32, (QL, QL), 0)
    lane = lax.broadcasted_iota(jnp.int32, (QL, QL), 1)
    return (row >> 6) == (lane >> 6)


def block_diagonal(rows128, group, mask):
    lane = lax.broadcasted_iota(jnp.int32, rows128.shape, 1)
    other = pltpu.roll(rows128, 64, 1)
    keep = (lane < 64) if group == 0 else (lane >= 64)
    twice = jnp.where(keep, rows128, other)
    wide = jnp.concatenate([twice, twice], axis=1)
    tall = jnp.concatenate([wide] * 4, axis=0)
    return jnp.where(mask, tall, 0.0).astype(BF)


def fold_diagonal(products, mask):
    kept = jnp.where(mask, products, 0.0)
    tall = kept[0:64] + kept[64:128] + kept[128:192] + kept[192:256]
    pair = tall[:, :128] + tall[:, 128:]
    return pair + pltpu.roll(pair, 64, 1)


def pack_kernel(place, wq_ref, wo_ref, gain_ref, out_ref):
    out_ref[:, :QKVW] = wq_ref[0]
    out_ref[0:32, QKVW : QKVW + 1024] = wo_ref[0, :, :1024]
    out_ref[32:64, QKVW : QKVW + 1024] = wo_ref[0, :, 1024:]
    gain = gain_ref[...].astype(F32)
    zero = jnp.zeros_like(gain)
    low = jnp.concatenate([gain, zero], axis=1)
    high = jnp.concatenate([zero, gain], axis=1)
    pair = jnp.where(place[CORE] == 0, low, high)
    out_ref[:, QKVW + 1024 :] = jnp.broadcast_to(pair, (64, 128)).astype(BF)


def pack(place, wq, wo, gain):
    return pl.pallas_call(
        pack_kernel,
        out_shape=pltpu.VMEM((64, PACKW), BF),
        in_specs=[SM, VM, VM, VM],
        out_specs=VM,
        compiler_params=pltpu.CompilerParams(vmem_limit_bytes=SMALL_LIMIT),
        name="pack",
    )(place, wq, wo, gain)


def forward_kernel(relative, place, lengths, x_ref, cos_ref, sin_ref, *refs):
    pieces = refs[:32]
    (wq_ref, wo_ref, gain_ref, scale_ref, probs_ref, q_ref, bdk_ref, bdv_ref,
     normed_mine, normed_other, attended_mine, attended_other, gain_pieces) = refs[32:]
    for i, piece in enumerate(pieces):
        swap_x, step, swap_core = relative[i]
        owner = dp_index(place[XP] ^ swap_x, (place[ZP] + step) & 7, place[CORE] ^ swap_core)
        row64 = pl.multiple_of(owner * 64, 64)
        row32 = pl.multiple_of(owner * 32, 32)
        row16 = pl.multiple_of(owner * 16, 16)
        gain_pieces[pl.ds(row16, 16), :] = piece[0:16, QKVW + 1024 :]
        wq_ref[pl.ds(row64, 64), :] = piece[:, :QKVW]
        wo_ref[pl.ds(row32, 32), pl.ds(0, 1024)] = piece[0:32, QKVW : QKVW + 1024]
        wo_ref[pl.ds(row32, 32), pl.ds(1024, 1024)] = piece[32:64, QKVW : QKVW + 1024]
    wide = x_ref[...].astype(F32)
    inverse = lax.rsqrt(jnp.sum(wide * wide, axis=1, keepdims=True) * (1.0 / D) + EPSILON)
    scale_ref[...] = jnp.broadcast_to(inverse, (TOK, 128))
    mask = block_diagonal_mask()
    attended = {}
    for i in range(16):
        both = (gain_pieces[pl.ds(32 * i, 1), :].astype(F32)
                + gain_pieces[pl.ds(32 * i + 16, 1), :].astype(F32))
        gain_ref[:, pl.ds(128 * i, 128)] = jnp.broadcast_to(both, (8, 128))
    normed = (wide * inverse * gain_ref[0:1, :]).astype(BF)
    right = place[XP] == 1
    for i in range(NZ):
        low = normed[:, i * 128 : (i + 1) * 128]
        high = normed[:, 1024 + i * 128 : 1024 + (i + 1) * 128]
        normed_mine[i] = jnp.where(right, high, low)
        normed_other[i] = jnp.where(right, low, high)
    projected = nn(normed, wq_ref[...])
    cosine = cos_ref[...]
    sine = sin_ref[...]
    queries = rotate(projected[:, :QW], cosine, sine).astype(BF)
    keys = rotate(projected[:, QW : QW + KVW], cosine, sine).astype(BF).astype(F32)
    values = projected[:, QW + KVW :].astype(BF).astype(F32)
    row = lax.broadcasted_iota(jnp.int32, (NB, QL), 0)
    lane = lax.broadcasted_iota(jnp.int32, (NB, QL), 1) & 63
    for m in range(MB):
        rows = slice(m * NB, (m + 1) * NB)
        length = jnp.where(row < SEQLEN, lengths[2 * m], lengths[2 * m + 1])
        allowed = ((row >> 5) == (lane >> 5)) & (lane <= row) & ((lane & 31) < length)
        for g in range(2):
            bdk = block_diagonal(keys[rows], g, mask)
            bdv = block_diagonal(values[rows], g, mask)
            bdk_ref[m, g] = bdk
            bdv_ref[m, g] = bdv
            for t in (2 * g, 2 * g + 1):
                quad = queries[rows, t * QL : (t + 1) * QL]
                q_ref[m, pl.ds(t * NB, NB), :] = quad
                scores = nt(quad, bdk) * 0.125
                terms = jnp.where(allowed, jnp.exp(jnp.where(allowed, scores, 0.0)), 0.0)
                probs = terms / half_sums(terms)
                probs_ref[m, pl.ds(t * NB, NB), :] = probs
                got = nn(probs.astype(BF), bdv).astype(BF)
                attended[t] = got
        for i in range(2):
            low, high = attended[i], attended[2 + i]
            attended_mine[rows, i * QL : (i + 1) * QL] = jnp.where(right, high, low)
            attended_other[rows, i * QL : (i + 1) * QL] = jnp.where(right, low, high)


def forward(relative, place, lengths, inputs, cosine, sine, pieces):
    shapes = [
        ((D, QKVW), BF), ((QW, D), BF), ((8, D), F32), ((TOK, 128), F32),
        ((MB, QUADS * NB, QL), F32), ((MB, QUADS * NB, QL), BF),
        ((MB, 2, QL, QL), BF), ((MB, 2, QL, QL), BF),
        ((NZ, TOK, 128), BF), ((NZ, TOK, 128), BF), ((TOK, 512), BF), ((TOK, 512), BF),
    ]
    return pl.pallas_call(
        partial(forward_kernel, relative),
        out_shape=[pltpu.VMEM(s, t) for s, t in shapes],
        in_specs=[SM, SM, VM, VM, VM] + [VM] * 32,
        out_specs=[VM] * len(shapes),
        scratch_shapes=[pltpu.VMEM((NDP * 16, 128), BF)],
        compiler_params=pltpu.CompilerParams(vmem_limit_bytes=VMEM_LIMIT),
        name="forward",
    )(place, lengths, inputs, cosine, sine, *[held(p) for p in pieces])


def tick_kernel(hop, m, *refs):
    (place, x_ref, gain_ref, scale_ref, wq_ref, wo_ref, probs_ref, q_ref, bdk_ref, bdv_ref,
     cos_ref, sin_ref, cot_ref) = refs[:13]
    last = hop == LAYERS - 1
    if last:
        gi_ref, gp_ref = refs[-2:]
    else:
        out_ref, gi_ref, gp_ref, keep_ref = refs[-4:]
    rows_m = slice(m * NB, (m + 1) * NB)

    @pl.when(place[SEC] == LAYERS - 1 - hop)
    def _():
        cot = cot_ref[rows_m, :] if hop == 0 else cot_ref[...]
        grad_att = nt(cot, wo_ref[...]).astype(BF)
        mask = block_diagonal_mask()
        cosine = cos_ref[pl.ds(0, NB), :]
        sine = -sin_ref[pl.ds(0, NB), :]
        parts = []
        grad_keys = []
        grad_values = []
        for g in range(2):
            bdk = bdk_ref[m, g]
            bdv = bdv_ref[m, g]
            rows = pl.ds(g * 2 * NB, 2 * NB)
            quads = jnp.concatenate(
                [grad_att[:, (2 * g + i) * QL : (2 * g + i + 1) * QL] for i in range(2)], axis=0)
            probs = probs_ref[m, rows, :]
            grad_probs = nt(quads, bdv)
            centre = half_sums(probs * grad_probs)
            grad_scores = (probs * (grad_probs - centre) * 0.125).astype(BF)
            grad_q = nn(grad_scores, bdk)
            parts.append(grad_q[:NB])
            parts.append(grad_q[NB:])
            grad_keys.append(fold_diagonal(tn(grad_scores, q_ref[m, rows, :]), mask))
            grad_values.append(fold_diagonal(tn(probs.astype(BF), quads), mask))
        lane = lax.broadcasted_iota(jnp.int32, (NB, 128), 1)
        key_rows = jnp.where(lane < 64, grad_keys[0], grad_keys[1])
        value_rows = jnp.where(lane < 64, grad_values[0], grad_values[1])
        rotated = rotate(jnp.concatenate(parts + [key_rows], axis=1), cosine, sine)
        gp = jnp.concatenate([rotated, value_rows], axis=1).astype(BF)
        gp_ref[...] = gp
        if not last:
            keep_ref[...] = cot
        grad_hat = nt(gp, wq_ref[...]) * gain_ref[0:1, :]
        wide = x_ref[rows_m, :].astype(F32)
        inverse = scale_ref[rows_m, 0:1]
        mean = jnp.sum(grad_hat * wide, axis=1, keepdims=True) * (1.0 / D)
        inner = inverse * (grad_hat - wide * (inverse * inverse * mean))
        grads = (cot.astype(F32) + inner).astype(BF)
        gi_ref[m] = grads
        if not last:
            out_ref[...] = grads


def tick(hop, m, place, fixed, cot, grads, kept):
    args = [held(v) for v in fixed] + [cot]
    last = hop == LAYERS - 1
    outs = [pltpu.VMEM((MB, NB, D), BF), pltpu.VMEM((NB, QKVW), BF), pltpu.VMEM((NB, D), BF)]
    state = [grads] + (list(kept) if kept else [None, None])
    if last:
        outs, state = outs[:2], state[:2]
    else:
        outs, state = [jax.ShapeDtypeStruct((NB, D), BF)] + outs, [None] + state
    aliases = {}
    for i, value in enumerate(state):
        if value is not None:
            aliases[1 + len(args)] = i
            args.append(held(value))
    return pl.pallas_call(
        partial(tick_kernel, hop, m),
        out_shape=outs,
        in_specs=[SM] + [VM] * len(args),
        out_specs=[VM] * len(outs),
        input_output_aliases=aliases,
        compiler_params=pltpu.CompilerParams(vmem_limit_bytes=VMEM_LIMIT),
        name="tick",
    )(place, *args)


def last_cot_kernel(place, incoming, cot_ref, out_ref):
    out_ref[...] = jnp.where(place[SEC] == 0, incoming[...], cot_ref[...])


def last_cot(place, incoming, cot):
    return pl.pallas_call(
        last_cot_kernel,
        out_shape=pltpu.VMEM((NB, D), BF),
        in_specs=[SM, VM, VM],
        out_specs=VM,
        compiler_params=pltpu.CompilerParams(vmem_limit_bytes=SMALL_LIMIT),
        name="last_cot",
    )(place, incoming, held(cot))


def columns(refs, core, width):
    first = pl.multiple_of(core * width, width)
    return jnp.concatenate([r[:, pl.ds(first, width)] for r in refs], axis=0)


def qkv_terms_kernel(place, *refs):
    normed = refs[:4]
    outs = refs[12:]
    right = columns(refs[4:12], place[CORE], 640)
    for k in range(NZ):
        chunk = (place[ZP] + k) & 7
        left = jnp.concatenate([r[chunk] for r in normed], axis=0)
        outs[k][...] = tn(left, right).astype(BF)


def out_terms_kernel(place, *refs):
    outs = refs[12:20]
    scratch = refs[20]
    left = jnp.concatenate([r[...] for r in refs[:4]], axis=0)
    total = tn(left, columns(refs[4:12], place[CORE], 1024)).astype(BF)
    for z in range(NZ):
        scratch[z] = total[z * 64 : (z + 1) * 64]
    for k in range(NZ):
        outs[k][...] = scratch[(place[ZP] + k) & 7]


def qkv_terms(place, normed, gp):
    return pl.pallas_call(
        qkv_terms_kernel,
        out_shape=[jax.ShapeDtypeStruct((128, 640), BF)] * NZ,
        in_specs=[SM] + [VM] * 12,
        out_specs=[VM] * NZ,
        compiler_params=pltpu.CompilerParams(vmem_limit_bytes=VMEM_LIMIT),
        name="qkv_terms",
    )(place, *normed, *gp)


def out_terms(place, attended, cot):
    return pl.pallas_call(
        out_terms_kernel,
        out_shape=[jax.ShapeDtypeStruct((64, 1024), BF)] * NZ,
        in_specs=[SM] + [VM] * 12,
        out_specs=[VM] * NZ,
        scratch_shapes=[pltpu.VMEM((NZ, 64, 1024), BF)],
        compiler_params=pltpu.CompilerParams(vmem_limit_bytes=VMEM_LIMIT),
        name="out_terms",
    )(place, *attended, *cot)


def add_kernel(place, *refs):
    kept, other = refs[-2:]
    total = refs[0][...].astype(F32)
    for r in refs[1:-2]:
        total = total + r[...].astype(F32)
    half = total.shape[0] // 2
    first = place[CORE] == 0
    kept[...] = jnp.where(first, total[:half], total[half:])
    other[...] = jnp.where(first, total[half:], total[:half])


def add_terms(place, parts):
    rows, width = parts[0].shape
    return pl.pallas_call(
        add_kernel,
        out_shape=[jax.ShapeDtypeStruct((rows // 2, width), F32)] * 2,
        in_specs=[SM] + [VM] * len(parts),
        out_specs=[VM] * 2,
        compiler_params=pltpu.CompilerParams(vmem_limit_bytes=SMALL_LIMIT),
        name="add_terms",
    )(place, *parts)


def join(place, kept, other):
    first = place[CORE] == 0
    left = jnp.where(first, kept[...], other[...])
    right = jnp.where(first, other[...], kept[...])
    return jnp.concatenate([left, right], axis=1)


def finish_out_kernel(place, kept, other, out_ref):
    out_ref[0] = join(place, kept, other)


def finish_qkv_kernel(place, kept, other, wq_ref, gain_ref, out_ref, gain_out):
    total = join(place, kept, other)
    out_ref[0] = total
    column = jnp.sum(total * wq_ref[0].astype(F32), axis=1, keepdims=True)
    row = lax.broadcasted_iota(jnp.int32, (64, 64), 0)
    lane = lax.broadcasted_iota(jnp.int32, (64, 64), 1)
    sums = jnp.sum(jnp.where(row == lane, column, 0.0), axis=0, keepdims=True)
    gain_out[...] = sums / gain_ref[...].astype(F32)


def finish(kernel, shapes, name, place, *args):
    return pl.pallas_call(
        kernel,
        out_shape=[jax.ShapeDtypeStruct(s, F32) for s in shapes],
        in_specs=[SM] + [VM] * len(args),
        out_specs=[VM] * len(shapes),
        compiler_params=pltpu.CompilerParams(vmem_limit_bytes=SMALL_LIMIT),
        name=name,
    )(place, *args)


def tables():
    half = HD // 2
    inverse_freq = ROPE_BASE ** (-(np.arange(half) * 2.0 / HD))
    angles = np.arange(SEQLEN)[:, None] * inverse_freq[None, :]
    sine = np.sin(angles)
    cosine = np.tile(np.cos(angles), (TOK // SEQLEN, 4))
    sine = np.tile(np.concatenate([-sine, sine], axis=1), (TOK // SEQLEN, 2))
    return jnp.asarray(cosine, F32), jnp.asarray(sine, F32)


def dp_index(x, z, c):
    return (x * NZ + z) * 2 + c


def along_z(value, steps):
    return lax.ppermute(value, "dp", [
        (dp_index(x, z, c), dp_index(x, (z + steps) % NZ, c))
        for x in range(2) for z in range(NZ) for c in range(2)])


def across_x(value):
    return lax.ppermute(value, "dp", [(i, i ^ 16) for i in range(NDP)])


def across_core(value):
    return lax.ppermute(value, "dp", [(i, i ^ 1) for i in range(NDP)])


def body(stashed, grad_top, lengths, norm_gain, qkv_weight, out_weight):
    dp = lax.axis_index("dp")
    place = jnp.stack([lax.axis_index("section"), dp // 16, (dp // 2) % NZ, dp % 2]).astype(jnp.int32)

    packed = pack(place, qkv_weight, out_weight, norm_gain)
    own = [packed, across_x(packed)]
    pieces = [(own[0], 0, 0), (own[1], 1, 0)]
    up, down = list(own), list(own)
    for k in range(1, 4):
        up = [along_z(v, 1) for v in up]
        down = [along_z(v, -1) for v in down]
        for s in range(2):
            pieces.append((up[s], s, -k))
            pieces.append((down[s], s, k))
    pieces.append((along_z(up[0], 1), 0, 4))
    pieces.append((along_z(down[1], -1), 1, 4))
    arrays = [p[0] for p in pieces] + [across_core(p[0]) for p in pieces]
    relative = [(s, dz, c) for c in range(2) for _, s, dz in pieces]
    cosine, sine = tables()
    inputs = stashed[0]
    (wq, wo, gain_row, scale, probs, q, bdk, bdv, normed, normed_other, attended, attended_other) = forward(
        relative, place, lengths, inputs, cosine, sine, arrays)
    fixed = (inputs, gain_row, scale, wq, wo, probs, q, bdk, bdv, cosine, sine)

    def gathered(mine, theirs):
        other = across_x(theirs)
        return [mine, other, across_core(mine), across_core(other)]

    def with_cores(own, crossed):
        mine = own + crossed
        return mine + [across_core(v) for v in mine]

    normed_blocks = gathered(normed, normed_other)
    attended_blocks = gathered(attended, attended_other)

    arriving = [grad_top] * MB
    kept = [None] * MB
    grads_in = None
    for hop in range(LAYERS - 1):
        for m in range(MB):
            out, grads_in, *kept[m] = tick(hop, m, place, fixed, arriving[m], grads_in, kept[m])
            arriving[m] = lax.ppermute(out, "section", [(LAYERS - 1 - hop, LAYERS - 2 - hop)])
    cots, gps, crossed_cots, crossed_gps = [], [], [], []
    for m in range(MB):
        cots.append(last_cot(place, arriving[m], kept[m][1]))
        crossed_cots.append(across_x(cots[m]))
        grads_in, gp = tick(LAYERS - 1, m, place, fixed, arriving[m], grads_in, kept[m])
        gps.append(gp)
        crossed_gps.append(across_x(gp))
    crossed_cots[0], crossed_cots[1], crossed_gps[0], _ = lax.optimization_barrier(
        (crossed_cots[0], crossed_cots[1], crossed_gps[0], gps[1]))
    out_chunks = out_terms(place, attended_blocks, with_cores(cots, crossed_cots))
    crossed_gps[1], _ = lax.optimization_barrier((crossed_gps[1], out_chunks[0]))
    qkv_chunks = qkv_terms(place, normed_blocks, with_cores(gps, crossed_gps))

    def added(a, b):
        return (a.astype(F32) + b.astype(F32)).astype(BF)

    def summed(chunks):
        half = chunks[4].shape[0] // 2
        up, down = along_z(chunks[4][:half], 1), along_z(chunks[4][half:], -1)
        up = jnp.concatenate([added(up, chunks[3][:half]), chunks[3][half:]], axis=0)
        down = jnp.concatenate([chunks[5][:half], added(down, chunks[5][half:])], axis=0)
        for k in (2, 1, 0):
            up, down = along_z(up, 1), along_z(down, -1)
            if k:
                up, down = added(up, chunks[k]), added(down, chunks[8 - k])
        kept, other = add_terms(place, [chunks[0], up, down])
        return kept, across_core(other)

    out_grad, = finish(finish_out_kernel, [(1, 32, D)], "finish_out", place, *summed(out_chunks))
    qkv_grad, gain_grad = finish(
        finish_qkv_kernel, [(1, 64, QKVW), (1, 64)], "finish_qkv", place, *summed(qkv_chunks), qkv_weight, norm_gain)
    return (grads_in.reshape(1, TOK, D), gain_grad, qkv_grad, out_grad)


def solution(mesh):
    in_specs = (
        P("section", "dp", None),
        P("dp", None),
        P("dp"),
        P("section", "dp"),
        P("section", "dp", None),
        P("section", "dp", None),
    )
    out_specs = (
        P("section", "dp", None),
        P("section", "dp"),
        P("section", "dp", None),
        P("section", "dp", None),
    )
    return jax.shard_map(body, mesh=mesh, in_specs=in_specs, out_specs=out_specs, check_vma=False)
```

```python
from functools import partial

import jax
import jax.numpy as jnp
import numpy as np
from jax import lax
from jax.experimental import pallas as pl
from jax.experimental.pallas import tpu as pltpu
from jax.sharding import PartitionSpec as P

D = 2048
HD = 64
SEQLEN = 32
QW = 1024
KVW = 128
QKVW = 1280
TOK = 128
MB = 2
NB = TOK // MB
LAYERS = 8
NZ = 8
NDP = 32
QUADS = 4
QL = 256
EPSILON = 1e-05
ROPE_BASE = 10000.0
BF = jnp.bfloat16
F32 = jnp.float32
VMEM_LIMIT = 28 << 20
SMALL_LIMIT = 12 << 20
SEC, XP, ZP, CORE = range(4)
PACKW = QKVW + 1024 + 128

ANY = pl.BlockSpec(memory_space=pl.ANY)
VM = pl.BlockSpec(memory_space=pltpu.VMEM)
SM = pl.BlockSpec(memory_space=pltpu.SMEM)


def held(value):
    return pltpu.with_memory_space_constraint(value, pltpu.VMEM)


def in_hbm(value):
    return pltpu.with_memory_space_constraint(value, pltpu.HBM)


def nn(a, b):
    return lax.dot_general(a, b, (((1,), (0,)), ((), ())), preferred_element_type=F32)


def nt(a, b):
    return lax.dot_general(a, b, (((1,), (1,)), ((), ())), preferred_element_type=F32)


def tn(a, b):
    return lax.dot_general(a, b, (((0,), (0,)), ((), ())), preferred_element_type=F32)


def rotate(u, cosine, sine):
    rows = u.shape[0]
    lane = lax.broadcasted_iota(jnp.int32, (rows, 128), 1)
    first = (lane & 63) < 32
    parts = []
    for i in range(u.shape[1] // 128):
        block = u[:, i * 128 : (i + 1) * 128]
        swapped = jnp.where(first, pltpu.roll(block, 96, 1), pltpu.roll(block, 32, 1))
        parts.append(block * cosine + swapped * sine)
    return parts[0] if len(parts) == 1 else jnp.concatenate(parts, axis=1)


def half_sums(values):
    rows = values.shape[0]
    lane = lax.broadcasted_iota(jnp.int32, (rows, 128), 1)
    low = lane < 64
    parts = []
    for i in range(values.shape[1] // 128):
        block = values[:, i * 128 : (i + 1) * 128]
        left = jnp.sum(jnp.where(low, block, 0.0), axis=1, keepdims=True)
        right = jnp.sum(jnp.where(low, 0.0, block), axis=1, keepdims=True)
        parts.append(jnp.where(low, left, right))
    return jnp.concatenate(parts, axis=1)


def block_diagonal_mask():
    row = lax.broadcasted_iota(jnp.int32, (QL, QL), 0)
    lane = lax.broadcasted_iota(jnp.int32, (QL, QL), 1)
    return (row >> 6) == (lane >> 6)


def block_diagonal(rows128, group, mask):
    lane = lax.broadcasted_iota(jnp.int32, rows128.shape, 1)
    other = pltpu.roll(rows128, 64, 1)
    keep = (lane < 64) if group == 0 else (lane >= 64)
    twice = jnp.where(keep, rows128, other)
    wide = jnp.concatenate([twice, twice], axis=1)
    tall = jnp.concatenate([wide] * 4, axis=0)
    return jnp.where(mask, tall, 0.0).astype(BF)


def fold_diagonal(products, mask):
    kept = jnp.where(mask, products, 0.0)
    tall = kept[0:64] + kept[64:128] + kept[128:192] + kept[192:256]
    pair = tall[:, :128] + tall[:, 128:]
    return pair + pltpu.roll(pair, 64, 1)


def pack_kernel(place, wq_ref, wo_ref, gain_ref, out_ref, gain_own, sems):
    copies = [
        pltpu.make_async_copy(gain_ref, gain_own, sems.at[0]),
        pltpu.make_async_copy(wq_ref.at[0], out_ref.at[:, pl.ds(0, QKVW)], sems.at[1]),
        pltpu.make_async_copy(
            wo_ref.at[0, :, pl.ds(0, 1024)], out_ref.at[pl.ds(0, 32), pl.ds(QKVW, 1024)], sems.at[2]),
        pltpu.make_async_copy(
            wo_ref.at[0, :, pl.ds(1024, 1024)], out_ref.at[pl.ds(32, 32), pl.ds(QKVW, 1024)], sems.at[3]),
    ]
    for copy in copies:
        copy.start()
    copies[0].wait()
    gain = gain_own[...].astype(F32)
    zero = jnp.zeros_like(gain)
    low = jnp.concatenate([gain, zero], axis=1)
    high = jnp.concatenate([zero, gain], axis=1)
    pair = jnp.where(place[CORE] == 0, low, high)
    out_ref[:, QKVW + 1024 :] = jnp.broadcast_to(pair, (64, 128)).astype(BF)
    for copy in copies[1:]:
        copy.wait()


def pack(place, wq, wo, gain):
    return pl.pallas_call(
        pack_kernel,
        out_shape=pltpu.VMEM((64, PACKW), BF),
        in_specs=[SM, ANY, ANY, ANY],
        out_specs=VM,
        scratch_shapes=[pltpu.VMEM((1, 64), BF), pltpu.SemaphoreType.DMA((4,))],
        compiler_params=pltpu.CompilerParams(vmem_limit_bytes=SMALL_LIMIT),
        name="pack",
    )(place, in_hbm(wq), in_hbm(wo), in_hbm(gain))


def forward_kernel(relative, place, x_hbm, top_hbm, table_hbm, *refs):
    pieces = refs[:32]
    (x_ref, top_ref, table_ref, wqt_ref, wot_ref, gain_ref, scale_ref, probs_ref, q_ref, bdk_ref, bdv_ref,
     normed_mine, normed_other, attended_mine, attended_other,
     gain_pieces, wq_ref, wo_ref, sems) = refs[32:]
    copies = [
        pltpu.make_async_copy(source, target, sems.at[i])
        for i, (source, target) in enumerate(((x_hbm.at[0], x_ref), (table_hbm, table_ref), (top_hbm, top_ref)))
    ]
    for copy in copies:
        copy.start()
    for i, piece in enumerate(pieces):
        swap_x, step, swap_core = relative[i]
        owner = dp_index(place[XP] ^ swap_x, (place[ZP] + step) & 7, place[CORE] ^ swap_core)
        row64 = pl.multiple_of(owner * 64, 64)
        row32 = pl.multiple_of(owner * 32, 32)
        row16 = pl.multiple_of(owner * 16, 16)
        gain_pieces[pl.ds(row16, 16), :] = piece[0:16, QKVW + 1024 :]
        wq_ref[pl.ds(row64, 64), :] = piece[:, :QKVW]
        wo_ref[pl.ds(row32, 32), pl.ds(0, 1024)] = piece[0:32, QKVW : QKVW + 1024]
        wo_ref[pl.ds(row32, 32), pl.ds(1024, 1024)] = piece[32:64, QKVW : QKVW + 1024]
    copies[0].wait()
    wide = x_ref[...].astype(F32)
    inverse = lax.rsqrt(jnp.sum(wide * wide, axis=1, keepdims=True) * (1.0 / D) + EPSILON)
    scale_ref[...] = jnp.broadcast_to(inverse, (TOK, 128))
    mask = block_diagonal_mask()
    attended = {}
    for i in range(16):
        both = (gain_pieces[pl.ds(32 * i, 1), :].astype(F32)
                + gain_pieces[pl.ds(32 * i + 16, 1), :].astype(F32))
        gain_ref[:, pl.ds(128 * i, 128)] = jnp.broadcast_to(both, (8, 128))
    normed = (wide * inverse * gain_ref[0:1, :]).astype(BF)
    right = place[XP] == 1
    for i in range(NZ):
        low = normed[:, i * 128 : (i + 1) * 128]
        high = normed[:, 1024 + i * 128 : 1024 + (i + 1) * 128]
        normed_mine[i] = jnp.where(right, high, low)
        normed_other[i] = jnp.where(right, low, high)
    projected = nn(normed, wq_ref[...])
    for i in range(8):
        wqt_ref[:, i * 256 : (i + 1) * 256] = wq_ref[i * 256 : (i + 1) * 256, :].T
    for i in range(4):
        wot_ref[:, i * 256 : (i + 1) * 256] = wo_ref[i * 256 : (i + 1) * 256, :].T
    copies[1].wait()
    cosine = table_ref[:, :128]
    sine = table_ref[:, 128:]
    queries = rotate(projected[:, :QW], cosine, sine).astype(BF)
    keys = rotate(projected[:, QW : QW + KVW], cosine, sine).astype(BF).astype(F32)
    values = projected[:, QW + KVW :].astype(BF).astype(F32)
    row = lax.broadcasted_iota(jnp.int32, (NB, QL), 0)
    lane = lax.broadcasted_iota(jnp.int32, (NB, QL), 1) & 63
    for m in range(MB):
        rows = slice(m * NB, (m + 1) * NB)
        length = jnp.where(row < SEQLEN, place[4 + 2 * m], place[5 + 2 * m])
        allowed = ((row >> 5) == (lane >> 5)) & (lane <= row) & ((lane & 31) < length)
        for g in range(2):
            bdk = block_diagonal(keys[rows], g, mask)
            bdv = block_diagonal(values[rows], g, mask)
            bdk_ref[m, g] = bdk
            bdv_ref[m, g] = bdv
            for t in (2 * g, 2 * g + 1):
                quad = queries[rows, t * QL : (t + 1) * QL]
                q_ref[m, pl.ds(t * NB, NB), :] = quad
                scores = nt(quad, bdk) * 0.125
                terms = jnp.where(allowed, jnp.exp(jnp.where(allowed, scores, 0.0)), 0.0)
                probs = terms / half_sums(terms)
                probs_ref[m, pl.ds(t * NB, NB), :] = probs
                got = nn(probs.astype(BF), bdv).astype(BF)
                attended[t] = got
        for i in range(2):
            low, high = attended[i], attended[2 + i]
            attended_mine[rows, i * QL : (i + 1) * QL] = jnp.where(right, high, low)
            attended_other[rows, i * QL : (i + 1) * QL] = jnp.where(right, low, high)
    copies[2].wait()


def forward(relative, place, inputs, top, table, pieces):
    shapes = [
        ((TOK, D), BF), ((TOK, D), BF), ((TOK, 256), F32), ((QKVW, D), BF), ((D, QW), BF), ((8, D), F32),
        ((TOK, 128), F32), ((MB, QUADS * NB, QL), F32), ((MB, QUADS * NB, QL), BF),
        ((MB, 2, QL, QL), BF), ((MB, 2, QL, QL), BF),
        ((NZ, TOK, 128), BF), ((NZ, TOK, 128), BF), ((TOK, 512), BF), ((TOK, 512), BF),
    ]
    return pl.pallas_call(
        partial(forward_kernel, relative),
        out_shape=[pltpu.VMEM(s, t) for s, t in shapes],
        in_specs=[SM, ANY, ANY, ANY] + [VM] * 32,
        out_specs=[VM] * len(shapes),
        scratch_shapes=[
            pltpu.VMEM((NDP * 16, 128), BF), pltpu.VMEM((D, QKVW), BF), pltpu.VMEM((QW, D), BF),
            pltpu.SemaphoreType.DMA((3,))],
        compiler_params=pltpu.CompilerParams(vmem_limit_bytes=VMEM_LIMIT),
        name="forward",
    )(place, in_hbm(inputs), in_hbm(top), in_hbm(table), *[held(p) for p in pieces])


def tick_kernel(hop, m, *refs):
    (place, x_ref, gain_ref, scale_ref, wqt_ref, wot_ref, probs_ref, q_ref, bdk_ref, bdv_ref,
     table_ref, cot_ref) = refs[:12]
    last = hop == LAYERS - 1
    if last:
        gi_ref, gp_ref, final_ref = refs[-3:]
    else:
        out_ref, gi_ref, gp_ref, keep_ref = refs[-4:]
    rows_m = slice(m * NB, (m + 1) * NB)

    @pl.when(place[SEC] == LAYERS - 1 - hop)
    def _():
        if hop == 0:
            cot = cot_ref[rows_m, :]
        elif last and m == 1:
            cot = cot_ref[:, QKVW:]
        else:
            cot = cot_ref[...]
        grad_att = nn(cot, wot_ref[...]).astype(BF)
        mask = block_diagonal_mask()
        cosine = table_ref[0:NB, :128]
        sine = -table_ref[0:NB, 128:]
        parts = []
        grad_keys = []
        grad_values = []
        for g in range(2):
            bdk = bdk_ref[m, g]
            bdv = bdv_ref[m, g]
            rows = pl.ds(g * 2 * NB, 2 * NB)
            quads = jnp.concatenate(
                [grad_att[:, (2 * g + i) * QL : (2 * g + i + 1) * QL] for i in range(2)], axis=0)
            probs = probs_ref[m, rows, :]
            grad_probs = nt(quads, bdv)
            centre = half_sums(probs * grad_probs)
            grad_scores = (probs * (grad_probs - centre) * 0.125).astype(BF)
            grad_q = nn(grad_scores, bdk)
            parts.append(grad_q[:NB])
            parts.append(grad_q[NB:])
            grad_keys.append(fold_diagonal(tn(grad_scores, q_ref[m, rows, :]), mask))
            grad_values.append(fold_diagonal(tn(probs.astype(BF), quads), mask))
        lane = lax.broadcasted_iota(jnp.int32, (NB, 128), 1)
        key_rows = jnp.where(lane < 64, grad_keys[0], grad_keys[1])
        value_rows = jnp.where(lane < 64, grad_values[0], grad_values[1])
        rotated = rotate(jnp.concatenate(parts + [key_rows], axis=1), cosine, sine)
        gp = jnp.concatenate([rotated, value_rows], axis=1).astype(BF)
        gp_ref[m] = gp
        if not last:
            keep_ref[m] = cot
        grad_hat = nn(gp, wqt_ref[...]) * gain_ref[0:1, :]
        wide = x_ref[rows_m, :].astype(F32)
        inverse = scale_ref[rows_m, 0:1]
        mean = jnp.sum(grad_hat * wide, axis=1, keepdims=True) * (1.0 / D)
        inner = inverse * (grad_hat - wide * (inverse * inverse * mean))
        grads = (cot.astype(F32) + inner).astype(BF)
        gi_ref[m] = grads
        if not last:
            out_ref[...] = grads

    if last:
        final_ref[...] = gp_ref[m]


def tick(hop, m, place, fixed, cot, state):
    args = [held(v) for v in fixed] + [cot if hop else held(cot)]
    last = hop == LAYERS - 1
    outs = [pltpu.VMEM((MB, NB, w), BF) for w in (D, QKVW, D)]
    if last:
        outs = outs[:2] + [pltpu.VMEM((NB, QKVW), BF)]
    else:
        outs = [jax.ShapeDtypeStruct((NB, D), BF)] + outs
    aliases = {}
    for i, value in enumerate((state or [])[: 2 if last else 3]):
        aliases[1 + len(args)] = i if last else i + 1
        args.append(held(value))
    return pl.pallas_call(
        partial(tick_kernel, hop, m),
        out_shape=outs,
        in_specs=[SM] + [VM] * len(args),
        out_specs=[VM] * len(outs),
        input_output_aliases=aliases,
        compiler_params=pltpu.CompilerParams(vmem_limit_bytes=VMEM_LIMIT),
        name="tick",
    )(place, *args)


def first_cot_kernel(place, incoming, cot_ref, out_ref):
    out_ref[...] = jnp.where(place[SEC] == 0, incoming[...], cot_ref[0])


def first_cot(place, incoming, cot):
    return pl.pallas_call(
        first_cot_kernel,
        out_shape=pltpu.VMEM((NB, D), BF),
        in_specs=[SM, VM, VM],
        out_specs=VM,
        compiler_params=pltpu.CompilerParams(vmem_limit_bytes=SMALL_LIMIT),
        name="first_cot",
    )(place, incoming, held(cot))


def second_kernel(place, incoming, cot_ref, gp_ref, out_ref):
    out_ref[:, :QKVW] = gp_ref[0]
    out_ref[:, QKVW:] = jnp.where(place[SEC] == 0, incoming[...], cot_ref[1])


def second(place, incoming, cot, gp):
    return pl.pallas_call(
        second_kernel,
        out_shape=pltpu.VMEM((NB, QKVW + D), BF),
        in_specs=[SM, VM, VM, VM],
        out_specs=VM,
        compiler_params=pltpu.CompilerParams(vmem_limit_bytes=SMALL_LIMIT),
        name="second",
    )(place, incoming, held(cot), held(gp))


def columns(refs, core, width, start=0):
    first = pl.multiple_of(core * width, 128)
    return jnp.concatenate([r[:, pl.ds(first + (i % 2) * start, width)] for i, r in enumerate(refs)], axis=0)


def qkv_terms_kernel(place, *refs):
    normed = refs[:4]
    outs = refs[12:]
    right = columns(refs[4:12], place[CORE], 640)
    for k in range(NZ):
        chunk = (place[ZP] + k) & 7
        left = jnp.concatenate([r[chunk] for r in normed], axis=0)
        outs[k][...] = tn(left, right).astype(BF)


def out_terms_kernel(place, *refs):
    outs = refs[12:20]
    scratch = refs[20]
    left = jnp.concatenate([r[...] for r in refs[:4]], axis=0)
    total = tn(left, columns(refs[4:12], place[CORE], 1024, QKVW)).astype(BF)
    for z in range(NZ):
        scratch[z] = total[z * 64 : (z + 1) * 64]
    for k in range(NZ):
        outs[k][...] = scratch[(place[ZP] + k) & 7]


def qkv_terms(place, normed, gp):
    return pl.pallas_call(
        qkv_terms_kernel,
        out_shape=[jax.ShapeDtypeStruct((128, 640), BF)] * NZ,
        in_specs=[SM] + [VM] * 12,
        out_specs=[VM] * NZ,
        compiler_params=pltpu.CompilerParams(vmem_limit_bytes=VMEM_LIMIT),
        name="qkv_terms",
    )(place, *normed, *gp)


def out_terms(place, attended, cot):
    return pl.pallas_call(
        out_terms_kernel,
        out_shape=[jax.ShapeDtypeStruct((64, 1024), BF)] * NZ,
        in_specs=[SM] + [VM] * 12,
        out_specs=[VM] * NZ,
        scratch_shapes=[pltpu.VMEM((NZ, 64, 1024), BF)],
        compiler_params=pltpu.CompilerParams(vmem_limit_bytes=VMEM_LIMIT),
        name="out_terms",
    )(place, *attended, *cot)


def add_kernel(place, *refs):
    kept, other = refs[-2:]
    total = refs[0][...].astype(F32)
    for r in refs[1:-2]:
        total = total + r[...].astype(F32)
    half = total.shape[0] // 2
    first = place[CORE] == 0
    kept[...] = jnp.where(first, total[:half], total[half:])
    other[...] = jnp.where(first, total[half:], total[:half])


def add_terms(place, parts):
    rows, width = parts[0].shape
    return pl.pallas_call(
        add_kernel,
        out_shape=[jax.ShapeDtypeStruct((rows // 2, width), F32)] * 2,
        in_specs=[SM] + [VM] * len(parts),
        out_specs=[VM] * 2,
        compiler_params=pltpu.CompilerParams(vmem_limit_bytes=SMALL_LIMIT),
        name="add_terms",
    )(place, *parts)


def join(place, kept, other):
    first = place[CORE] == 0
    left = jnp.where(first, kept[...], other[...])
    right = jnp.where(first, other[...], kept[...])
    return jnp.concatenate([left, right], axis=1)


def finish_out_kernel(place, kept, other, out_ref):
    out_ref[0] = join(place, kept, other)


def finish_qkv_kernel(place, kept, other, wq_ref, gain_ref, out_ref, gain_out):
    total = join(place, kept, other)
    out_ref[0] = total
    column = jnp.sum(total * wq_ref[0].astype(F32), axis=1, keepdims=True)
    row = lax.broadcasted_iota(jnp.int32, (64, 64), 0)
    lane = lax.broadcasted_iota(jnp.int32, (64, 64), 1)
    sums = jnp.sum(jnp.where(row == lane, column, 0.0), axis=0, keepdims=True)
    gain_out[...] = sums / gain_ref[...].astype(F32)


def finish(kernel, shapes, name, place, *args):
    return pl.pallas_call(
        kernel,
        out_shape=[jax.ShapeDtypeStruct(s, F32) for s in shapes],
        in_specs=[SM] + [VM] * len(args),
        out_specs=[VM] * len(shapes),
        compiler_params=pltpu.CompilerParams(vmem_limit_bytes=SMALL_LIMIT),
        name=name,
    )(place, *args)


def tables():
    half = HD // 2
    inverse_freq = ROPE_BASE ** (-(np.arange(half) * 2.0 / HD))
    angles = np.arange(SEQLEN)[:, None] * inverse_freq[None, :]
    sine = np.sin(angles)
    cosine = np.tile(np.cos(angles), (TOK // SEQLEN, 4))
    sine = np.tile(np.concatenate([-sine, sine], axis=1), (TOK // SEQLEN, 2))
    return jnp.asarray(np.concatenate([cosine, sine], axis=1), F32)


def dp_index(x, z, c):
    return (x * NZ + z) * 2 + c


def along_z(value, steps):
    return lax.ppermute(value, "dp", [
        (dp_index(x, z, c), dp_index(x, (z + steps) % NZ, c))
        for x in range(2) for z in range(NZ) for c in range(2)])


def across_x(value):
    return lax.ppermute(value, "dp", [(i, i ^ 16) for i in range(NDP)])


def across_core(value):
    return lax.ppermute(value, "dp", [(i, i ^ 1) for i in range(NDP)])


def body(stashed, grad_top, lengths, norm_gain, qkv_weight, out_weight):
    dp = lax.axis_index("dp")
    place = jnp.stack([lax.axis_index("section"), dp // 16, (dp // 2) % NZ, dp % 2]).astype(jnp.int32)
    place = jnp.concatenate([place, lengths])

    packed = pack(place, qkv_weight, out_weight, norm_gain)
    crossed = across_x(packed)
    up, down = [packed], [packed]
    for k in range(1, 5):
        up.append(along_z(up[-1], 1))
    for k in range(1, 4):
        down.append(along_z(down[-1], -1))
    far_up, far_down = across_x(up[2]), across_x(down[2])
    pieces = [(packed, 0, 0), (crossed, 1, 0)]
    pieces += [(up[k], 0, -k) for k in range(1, 5)] + [(down[k], 0, k) for k in range(1, 4)]
    pieces += [(along_z(crossed, 1), 1, -1), (along_z(crossed, -1), 1, 1), (far_up, 1, -2), (far_down, 1, 2)]
    pieces += [(along_z(far_up, 1), 1, -3), (along_z(far_down, -1), 1, 3), (across_x(up[4]), 1, 4)]
    arrays = [p[0] for p in pieces] + [across_core(p[0]) for p in pieces]
    relative = [(s, dz, c) for c in range(2) for _, s, dz in pieces]
    (inputs, top, table, wqt, wot, gain_row, scale, probs, q, bdk, bdv,
     normed, normed_other, attended, attended_other) = forward(
        relative, place, stashed, grad_top, tables(), arrays)
    fixed = (inputs, gain_row, scale, wqt, wot, probs, q, bdk, bdv, table)

    def gathered(mine, theirs):
        other = across_x(theirs)
        return [mine, other, across_core(mine), across_core(other)]

    def with_cores(own, crossed):
        mine = own + crossed
        return mine + [across_core(v) for v in mine]

    arriving = [top] * MB
    state = None
    for hop in range(LAYERS - 1):
        for m in range(MB):
            out, *state = tick(hop, m, place, fixed, arriving[m], state)
            arriving[m] = lax.ppermute(out, "section", [(LAYERS - 1 - hop, LAYERS - 2 - hop)])
        if hop == 0:
            normed_other, attended_other, normed, attended, state[0] = lax.optimization_barrier(
                (normed_other, attended_other, normed, attended, state[0]))
            blocks = gathered(normed, normed_other) + gathered(attended, attended_other)
        if hop == 3:
            *blocks, state[0] = lax.optimization_barrier((*blocks, state[0]))
    normed_blocks, attended_blocks = blocks[:4], blocks[4:]
    cot0 = first_cot(place, arriving[0], state[2])
    crossed_cot0 = across_x(cot0)
    grads_in, gp, _ = tick(LAYERS - 1, 0, place, fixed, cot0, state)
    mixed = second(place, arriving[1], state[2], gp)
    crossed_mixed = across_x(mixed)
    grads_in, _, gp1 = tick(LAYERS - 1, 1, place, fixed, mixed, [grads_in, gp])
    crossed_gp1 = across_x(gp1)
    cot0, mixed, gp1, crossed_cot0, crossed_mixed, crossed_gp1 = lax.optimization_barrier(
        (cot0, mixed, gp1, crossed_cot0, crossed_mixed, crossed_gp1))
    both = with_cores([cot0, mixed], [crossed_cot0, crossed_mixed])
    out_chunks = out_terms(place, attended_blocks, both)
    last = with_cores([gp1], [crossed_gp1])
    gps = [v for i in range(4) for v in (both[2 * i + 1], last[i])]
    qkv_chunks = qkv_terms(place, normed_blocks, gps)

    def added(a, b):
        return (a.astype(F32) + b.astype(F32)).astype(BF)

    def summed(chunks):
        half = chunks[4].shape[0] // 2
        up, down = along_z(chunks[4][:half], 1), along_z(chunks[4][half:], -1)
        up = jnp.concatenate([added(up, chunks[3][:half]), chunks[3][half:]], axis=0)
        down = jnp.concatenate([chunks[5][:half], added(down, chunks[5][half:])], axis=0)
        for k in (2, 1, 0):
            up, down = along_z(up, 1), along_z(down, -1)
            if k:
                up, down = added(up, chunks[k]), added(down, chunks[8 - k])
        kept, other = add_terms(place, [chunks[0], up, down])
        return kept, across_core(other)

    out_grad, = finish(finish_out_kernel, [(1, 32, D)], "finish_out", place, *summed(out_chunks))
    qkv_grad, gain_grad = finish(
        finish_qkv_kernel, [(1, 64, QKVW), (1, 64)], "finish_qkv", place, *summed(qkv_chunks), qkv_weight, norm_gain)
    return (grads_in.reshape(1, TOK, D), gain_grad, qkv_grad, out_grad)


def solution(mesh):
    in_specs = (
        P("section", "dp", None),
        P("dp", None),
        P("dp"),
        P("section", "dp"),
        P("section", "dp", None),
        P("section", "dp", None),
    )
    out_specs = (
        P("section", "dp", None),
        P("section", "dp"),
        P("section", "dp", None),
        P("section", "dp", None),
    )
    return jax.shard_map(body, mesh=mesh, in_specs=in_specs, out_specs=out_specs, check_vma=False)
```

```python
from functools import partial

import jax
import jax.numpy as jnp
import numpy as np
from jax import lax
from jax.experimental import pallas as pl
from jax.experimental.pallas import tpu as pltpu
from jax.sharding import PartitionSpec as P

D = 2048
HD = 64
SEQLEN = 32
QW = 1024
KVW = 128
QKVW = 1280
TOK = 128
MB = 4
NB = TOK // MB
LAYERS = 8
NZ = 8
NDP = 32
QUADS = 4
QL = 256
JL = 4 * NB
EPSILON = 1e-05
ROPE_BASE = 10000.0
BF = jnp.bfloat16
F32 = jnp.float32
VMEM_LIMIT = 28 << 20
SMALL_LIMIT = 12 << 20
SEC, XP, ZP, CORE = range(4)
PACKW = QKVW + 1024 + 128

ANY = pl.BlockSpec(memory_space=pl.ANY)
VM = pl.BlockSpec(memory_space=pltpu.VMEM)
SM = pl.BlockSpec(memory_space=pltpu.SMEM)


def held(value):
    return pltpu.with_memory_space_constraint(value, pltpu.VMEM)


def in_hbm(value):
    return pltpu.with_memory_space_constraint(value, pltpu.HBM)


def nn(a, b):
    return lax.dot_general(a, b, (((1,), (0,)), ((), ())), preferred_element_type=F32)


def nt(a, b):
    return lax.dot_general(a, b, (((1,), (1,)), ((), ())), preferred_element_type=F32)


def tn(a, b):
    return lax.dot_general(a, b, (((0,), (0,)), ((), ())), preferred_element_type=F32)


def rotate(u, cosine, sine):
    rows = u.shape[0]
    lane = lax.broadcasted_iota(jnp.int32, (rows, 128), 1)
    first = (lane & 63) < 32
    parts = []
    for i in range(u.shape[1] // 128):
        block = u[:, i * 128 : (i + 1) * 128]
        swapped = jnp.where(first, pltpu.roll(block, 96, 1), pltpu.roll(block, 32, 1))
        parts.append(block * cosine + swapped * sine)
    return parts[0] if len(parts) == 1 else jnp.concatenate(parts, axis=1)


def run_sums(values):
    rows = values.shape[0]
    run = lax.broadcasted_iota(jnp.int32, (rows, 128), 1) // NB
    parts = []
    for i in range(values.shape[1] // 128):
        block = values[:, i * 128 : (i + 1) * 128]
        out = jnp.zeros_like(block)
        for r in range(128 // NB):
            total = jnp.sum(jnp.where(run == r, block, 0.0), axis=1, keepdims=True)
            out = jnp.where(run == r, total, out)
        parts.append(out)
    return parts[0] if len(parts) == 1 else jnp.concatenate(parts, axis=1)


def block_diagonal_mask():
    row = lax.broadcasted_iota(jnp.int32, (JL, QL), 0)
    lane = lax.broadcasted_iota(jnp.int32, (JL, QL), 1)
    return (row // NB) == (lane >> 6)


def block_diagonal(rows128, group, mask):
    lane = lax.broadcasted_iota(jnp.int32, rows128.shape, 1)
    other = pltpu.roll(rows128, 64, 1)
    keep = (lane < 64) if group == 0 else (lane >= 64)
    twice = jnp.where(keep, rows128, other)
    wide = jnp.concatenate([twice, twice], axis=1)
    tall = jnp.concatenate([wide] * 4, axis=0)
    return jnp.where(mask, tall, 0.0).astype(BF)


def fold_diagonal(products, mask):
    kept = jnp.where(mask, products, 0.0)
    tall = kept[0:NB] + kept[NB : 2 * NB] + kept[2 * NB : 3 * NB] + kept[3 * NB :]
    pair = tall[:, :128] + tall[:, 128:]
    return pair + pltpu.roll(pair, 64, 1)


def pack_kernel(place, wq_ref, wo_ref, gain_ref, out_ref, gain_own, sems):
    copies = [
        pltpu.make_async_copy(gain_ref, gain_own, sems.at[0]),
        pltpu.make_async_copy(wq_ref.at[0], out_ref.at[:, pl.ds(0, QKVW)], sems.at[1]),
        pltpu.make_async_copy(
            wo_ref.at[0, :, pl.ds(0, 1024)], out_ref.at[pl.ds(0, 32), pl.ds(QKVW, 1024)], sems.at[2]),
        pltpu.make_async_copy(
            wo_ref.at[0, :, pl.ds(1024, 1024)], out_ref.at[pl.ds(32, 32), pl.ds(QKVW, 1024)], sems.at[3]),
    ]
    for copy in copies:
        copy.start()
    copies[0].wait()
    gain = gain_own[...].astype(F32)
    zero = jnp.zeros_like(gain)
    low = jnp.concatenate([gain, zero], axis=1)
    high = jnp.concatenate([zero, gain], axis=1)
    pair = jnp.where(place[CORE] == 0, low, high)
    out_ref[:, QKVW + 1024 :] = jnp.broadcast_to(pair, (64, 128)).astype(BF)
    for copy in copies[1:]:
        copy.wait()


def pack(place, wq, wo, gain):
    return pl.pallas_call(
        pack_kernel,
        out_shape=pltpu.VMEM((64, PACKW), BF),
        in_specs=[SM, ANY, ANY, ANY],
        out_specs=VM,
        scratch_shapes=[pltpu.VMEM((1, 64), BF), pltpu.SemaphoreType.DMA((4,))],
        compiler_params=pltpu.CompilerParams(vmem_limit_bytes=SMALL_LIMIT),
        name="pack",
    )(place, in_hbm(wq), in_hbm(wo), in_hbm(gain))


def forward_kernel(relative, place, x_hbm, top_hbm, table_hbm, *refs):
    pieces = refs[:32]
    (x_ref, top_ref, table_ref, wqt_ref, wot_ref, gain_ref, scale_ref, probs_ref, q_ref, bdk_ref, bdv_ref,
     mine_ref, other_ref,
     gain_pieces, wq_ref, wo_ref, sems) = refs[32:]
    copies = [
        pltpu.make_async_copy(source, target, sems.at[i])
        for i, (source, target) in enumerate(((x_hbm.at[0], x_ref), (table_hbm, table_ref), (top_hbm, top_ref)))
    ]
    for copy in copies:
        copy.start()
    for i, piece in enumerate(pieces):
        swap_x, step, swap_core = relative[i]
        owner = dp_index(place[XP] ^ swap_x, (place[ZP] + step) & 7, place[CORE] ^ swap_core)
        row64 = pl.multiple_of(owner * 64, 64)
        row32 = pl.multiple_of(owner * 32, 32)
        row16 = pl.multiple_of(owner * 16, 16)
        gain_pieces[pl.ds(row16, 16), :] = piece[0:16, QKVW + 1024 :]
        wq_ref[pl.ds(row64, 64), :] = piece[:, :QKVW]
        wo_ref[pl.ds(row32, 32), pl.ds(0, 1024)] = piece[0:32, QKVW : QKVW + 1024]
        wo_ref[pl.ds(row32, 32), pl.ds(1024, 1024)] = piece[32:64, QKVW : QKVW + 1024]
    copies[0].wait()
    wide = x_ref[...].astype(F32)
    inverse = lax.rsqrt(jnp.sum(wide * wide, axis=1, keepdims=True) * (1.0 / D) + EPSILON)
    scale_ref[...] = jnp.broadcast_to(inverse, (TOK, 128))
    mask = block_diagonal_mask()
    attended = {}
    for i in range(16):
        both = (gain_pieces[pl.ds(32 * i, 1), :].astype(F32)
                + gain_pieces[pl.ds(32 * i + 16, 1), :].astype(F32))
        gain_ref[:, pl.ds(128 * i, 128)] = jnp.broadcast_to(both, (8, 128))
    normed = (wide * inverse * gain_ref[0:1, :]).astype(BF)
    right = place[XP] == 1
    for i in range(NZ):
        low = normed[:, i * 128 : (i + 1) * 128]
        high = normed[:, 1024 + i * 128 : 1024 + (i + 1) * 128]
        mine_ref[i] = jnp.where(right, high, low)
        other_ref[i] = jnp.where(right, low, high)
    projected = nn(normed, wq_ref[...])
    for i in range(8):
        wqt_ref[:, i * 256 : (i + 1) * 256] = wq_ref[i * 256 : (i + 1) * 256, :].T
    for i in range(4):
        wot_ref[:, i * 256 : (i + 1) * 256] = wo_ref[i * 256 : (i + 1) * 256, :].T
    copies[1].wait()
    cosine = table_ref[:, :128]
    sine = table_ref[:, 128:]
    queries = rotate(projected[:, :QW], cosine, sine).astype(BF)
    keys = rotate(projected[:, QW : QW + KVW], cosine, sine).astype(BF).astype(F32)
    values = projected[:, QW + KVW :].astype(BF).astype(F32)
    row = lax.broadcasted_iota(jnp.int32, (NB, JL), 0)
    lane = lax.broadcasted_iota(jnp.int32, (NB, JL), 1) & (NB - 1)
    for m in range(MB):
        rows = slice(m * NB, (m + 1) * NB)
        allowed = (lane <= row) & (lane < place[4 + m])
        for g in range(2):
            bdk = block_diagonal(keys[rows], g, mask)
            bdv = block_diagonal(values[rows], g, mask)
            bdk_ref[m, g] = bdk
            bdv_ref[m, g] = bdv
            for t in (2 * g, 2 * g + 1):
                quad = queries[rows, t * QL : (t + 1) * QL]
                q_ref[m, pl.ds(t * NB, NB), :] = quad
                scores = nt(quad, bdk) * 0.125
                terms = jnp.where(allowed, jnp.exp(jnp.where(allowed, scores, 0.0)), 0.0)
                probs = terms / run_sums(terms)
                probs_ref[m, pl.ds(t * NB, NB), :] = probs
                got = nn(probs.astype(BF), bdv).astype(BF)
                attended[t] = got
        for i in range(2):
            low, high = attended[i], attended[2 + i]
            mine = jnp.where(right, high, low)
            other = jnp.where(right, low, high)
            for j in range(2):
                mine_ref[NZ + 2 * i + j, rows, :] = mine[:, j * 128 : (j + 1) * 128]
                other_ref[NZ + 2 * i + j, rows, :] = other[:, j * 128 : (j + 1) * 128]
    copies[2].wait()


def forward(relative, place, inputs, top, table, pieces):
    shapes = [
        ((TOK, D), BF), ((TOK, D), BF), ((TOK, 256), F32), ((QKVW, D), BF), ((D, QW), BF), ((8, D), F32),
        ((TOK, 128), F32), ((MB, QUADS * NB, JL), F32), ((MB, QUADS * NB, QL), BF),
        ((MB, 2, JL, QL), BF), ((MB, 2, JL, QL), BF),
        ((NZ + 4, TOK, 128), BF), ((NZ + 4, TOK, 128), BF),
    ]
    return pl.pallas_call(
        partial(forward_kernel, relative),
        out_shape=[pltpu.VMEM(s, t) for s, t in shapes],
        in_specs=[SM, ANY, ANY, ANY] + [VM] * 32,
        out_specs=[VM] * len(shapes),
        scratch_shapes=[
            pltpu.VMEM((NDP * 16, 128), BF), pltpu.VMEM((D, QKVW), BF), pltpu.VMEM((QW, D), BF),
            pltpu.SemaphoreType.DMA((3,))],
        compiler_params=pltpu.CompilerParams(vmem_limit_bytes=VMEM_LIMIT),
        name="forward",
    )(place, in_hbm(inputs), in_hbm(top), in_hbm(table), *[held(p) for p in pieces])


def handed_on(m):
    return {2: (0, 1, 2), 3: (3,)}.get(m, ())


def tick_kernel(hop, m, *refs):
    (place, x_ref, gain_ref, scale_ref, wqt_ref, wot_ref, probs_ref, q_ref, bdk_ref, bdv_ref,
     table_ref, cot_ref) = refs[:12]
    last = hop == LAYERS - 1
    if last:
        gi_ref, gp_ref, keep_ref, final_ref = refs[-4:]
    else:
        out_ref, gi_ref, gp_ref, keep_ref = refs[-4:]
    rows_m = slice(m * NB, (m + 1) * NB)

    @pl.when(place[SEC] == LAYERS - 1 - hop)
    def _():
        cot = cot_ref[rows_m, :] if hop == 0 else cot_ref[...]
        grad_att = nn(cot, wot_ref[...]).astype(BF)
        mask = block_diagonal_mask()
        cosine = table_ref[0:NB, :128]
        sine = -table_ref[0:NB, 128:]
        parts = []
        grad_keys = []
        grad_values = []
        for g in range(2):
            bdk = bdk_ref[m, g]
            bdv = bdv_ref[m, g]
            rows = pl.ds(g * 2 * NB, 2 * NB)
            quads = jnp.concatenate(
                [grad_att[:, (2 * g + i) * QL : (2 * g + i + 1) * QL] for i in range(2)], axis=0)
            probs = probs_ref[m, rows, :]
            grad_probs = nt(quads, bdv)
            centre = run_sums(probs * grad_probs)
            grad_scores = (probs * (grad_probs - centre) * 0.125).astype(BF)
            grad_q = nn(grad_scores, bdk)
            parts.append(grad_q[:NB])
            parts.append(grad_q[NB:])
            grad_keys.append(fold_diagonal(tn(grad_scores, q_ref[m, rows, :]), mask))
            grad_values.append(fold_diagonal(tn(probs.astype(BF), quads), mask))
        lane = lax.broadcasted_iota(jnp.int32, (NB, 128), 1)
        key_rows = jnp.where(lane < 64, grad_keys[0], grad_keys[1])
        value_rows = jnp.where(lane < 64, grad_values[0], grad_values[1])
        rotated = rotate(jnp.concatenate(parts + [key_rows], axis=1), cosine, sine)
        gp = jnp.concatenate([rotated, value_rows], axis=1).astype(BF)
        gp_ref[m] = gp
        keep_ref[m] = cot
        grad_hat = nn(gp, wqt_ref[...]) * gain_ref[0:1, :]
        wide = x_ref[rows_m, :].astype(F32)
        inverse = scale_ref[rows_m, 0:1]
        mean = jnp.sum(grad_hat * wide, axis=1, keepdims=True) * (1.0 / D)
        inner = inverse * (grad_hat - wide * (inverse * inverse * mean))
        grads = (cot.astype(F32) + inner).astype(BF)
        gi_ref[m] = grads
        if not last:
            out_ref[...] = grads

    if last:
        for i, source in enumerate(handed_on(m)):
            final_ref[i * NB : (i + 1) * NB, :QKVW] = gp_ref[source]
            final_ref[i * NB : (i + 1) * NB, QKVW:] = keep_ref[source]


def tick(hop, m, place, fixed, cot, state):
    args = [held(v) for v in fixed] + [cot if hop else held(cot)]
    last = hop == LAYERS - 1
    outs = [pltpu.VMEM((MB, NB, w), BF) for w in (D, QKVW, D)]
    if last:
        outs = outs + [pltpu.VMEM((max(1, len(handed_on(m))) * NB, QKVW + D), BF)]
    else:
        outs = [jax.ShapeDtypeStruct((NB, D), BF)] + outs
    aliases = {}
    for i, value in enumerate(state or []):
        aliases[1 + len(args)] = i if last else i + 1
        args.append(held(value))
    return pl.pallas_call(
        partial(tick_kernel, hop, m),
        out_shape=outs,
        in_specs=[SM] + [VM] * len(args),
        out_specs=[VM] * len(outs),
        input_output_aliases=aliases,
        compiler_params=pltpu.CompilerParams(vmem_limit_bytes=VMEM_LIMIT),
        name="tick",
    )(place, *args)


def columns(refs, core, width, start=0):
    first = pl.multiple_of(core * width, 128)
    return jnp.concatenate([r[:, pl.ds(first + start, width)] for r in refs], axis=0)


def qkv_terms_kernel(place, *refs):
    halves, payload = refs[:4], refs[4:12]
    grads, outs, grads_out, sem = refs[12], refs[13 : 13 + NZ], refs[-2], refs[-1]
    copy = pltpu.make_async_copy(grads, grads_out, sem.at[0])
    copy.start()
    right = columns(payload, place[CORE], 640)
    for k in range(NZ):
        chunk = (place[ZP] + k) & 7
        left = jnp.concatenate([r[chunk] for r in halves], axis=0)
        outs[k][...] = tn(left, right).astype(BF)
    copy.wait()


def out_terms_kernel(place, *refs):
    halves, payload = refs[:4], refs[4:12]
    outs, scratch = refs[12 : 12 + NZ], refs[-1]
    left = jnp.concatenate(
        [jnp.concatenate([r[NZ + j] for j in range(4)], axis=1) for r in halves], axis=0)
    total = tn(left, columns(payload, place[CORE], 1024, QKVW)).astype(BF)
    for z in range(NZ):
        scratch[z] = total[z * 64 : (z + 1) * 64]
    for k in range(NZ):
        outs[k][...] = scratch[(place[ZP] + k) & 7]


def qkv_terms(place, halves, payload, grads):
    *chunks, grads = pl.pallas_call(
        qkv_terms_kernel,
        out_shape=[jax.ShapeDtypeStruct((128, 640), BF)] * NZ + [pltpu.HBM((MB, NB, D), BF)],
        in_specs=[SM] + [VM] * 13,
        out_specs=[VM] * NZ + [ANY],
        scratch_shapes=[pltpu.SemaphoreType.DMA((1,))],
        compiler_params=pltpu.CompilerParams(vmem_limit_bytes=VMEM_LIMIT),
        name="qkv_terms",
    )(place, *halves, *payload, held(grads))
    return chunks, grads


def out_terms(place, halves, payload):
    return pl.pallas_call(
        out_terms_kernel,
        out_shape=[jax.ShapeDtypeStruct((64, 1024), BF)] * NZ,
        in_specs=[SM] + [VM] * 12,
        out_specs=[VM] * NZ,
        scratch_shapes=[pltpu.VMEM((NZ, 64, 1024), BF)],
        compiler_params=pltpu.CompilerParams(vmem_limit_bytes=VMEM_LIMIT),
        name="out_terms",
    )(place, *halves, *payload)


def add_kernel(place, *refs):
    first = place[CORE] == 0
    for i in range(2):
        own, up, down = refs[3 * i : 3 * i + 3]
        kept, other = refs[6 + 2 * i : 8 + 2 * i]
        total = own[...].astype(F32) + up[...].astype(F32) + down[...].astype(F32)
        half = total.shape[0] // 2
        kept[...] = jnp.where(first, total[:half], total[half:])
        other[...] = jnp.where(first, total[half:], total[:half])


def add_terms(place, parts):
    shapes = [(v.shape[0] // 2, v.shape[1]) for v in (parts[0], parts[0], parts[3], parts[3])]
    return pl.pallas_call(
        add_kernel,
        out_shape=[jax.ShapeDtypeStruct(s, F32) for s in shapes],
        in_specs=[SM] + [VM] * len(parts),
        out_specs=[VM] * len(shapes),
        compiler_params=pltpu.CompilerParams(vmem_limit_bytes=SMALL_LIMIT),
        name="add_terms",
    )(place, *parts)


def join(place, kept, other):
    first = place[CORE] == 0
    left = jnp.where(first, kept[...], other[...])
    right = jnp.where(first, other[...], kept[...])
    return jnp.concatenate([left, right], axis=1)


def finish_kernel(place, kept_qkv, other_qkv, kept_out, other_out, wq_ref, gain_ref, qkv_ref, out_ref, gain_out):
    out_ref[0] = join(place, kept_out, other_out)
    total = join(place, kept_qkv, other_qkv)
    qkv_ref[0] = total
    column = jnp.sum(total * wq_ref[0].astype(F32), axis=1, keepdims=True)
    row = lax.broadcasted_iota(jnp.int32, (64, 64), 0)
    lane = lax.broadcasted_iota(jnp.int32, (64, 64), 1)
    sums = jnp.sum(jnp.where(row == lane, column, 0.0), axis=0, keepdims=True)
    gain_out[...] = sums / gain_ref[...].astype(F32)


def finish(place, *args):
    shapes = [(1, 64, QKVW), (1, 32, D), (1, 64)]
    return pl.pallas_call(
        finish_kernel,
        out_shape=[jax.ShapeDtypeStruct(s, F32) for s in shapes],
        in_specs=[SM] + [VM] * len(args),
        out_specs=[VM] * len(shapes),
        compiler_params=pltpu.CompilerParams(vmem_limit_bytes=SMALL_LIMIT),
        name="finish",
    )(place, *args)


def tables():
    half = HD // 2
    inverse_freq = ROPE_BASE ** (-(np.arange(half) * 2.0 / HD))
    angles = np.arange(SEQLEN)[:, None] * inverse_freq[None, :]
    sine = np.sin(angles)
    cosine = np.tile(np.cos(angles), (TOK // SEQLEN, 4))
    sine = np.tile(np.concatenate([-sine, sine], axis=1), (TOK // SEQLEN, 2))
    return jnp.asarray(np.concatenate([cosine, sine], axis=1), F32)


def dp_index(x, z, c):
    return (x * NZ + z) * 2 + c


def along_z(value, steps):
    return lax.ppermute(value, "dp", [
        (dp_index(x, z, c), dp_index(x, (z + steps) % NZ, c))
        for x in range(2) for z in range(NZ) for c in range(2)])


def across_x(value):
    return lax.ppermute(value, "dp", [(i, i ^ 16) for i in range(NDP)])


def across_core(value):
    return lax.ppermute(value, "dp", [(i, i ^ 1) for i in range(NDP)])


def body(stashed, grad_top, lengths, norm_gain, qkv_weight, out_weight):
    dp = lax.axis_index("dp")
    place = jnp.stack([lax.axis_index("section"), dp // 16, (dp // 2) % NZ, dp % 2]).astype(jnp.int32)
    place = jnp.concatenate([place, lengths])

    packed = pack(place, qkv_weight, out_weight, norm_gain)
    crossed = across_x(packed)
    up, down = [packed], [packed]
    for k in range(1, 5):
        up.append(along_z(up[-1], 1))
    for k in range(1, 4):
        down.append(along_z(down[-1], -1))
    far_up, far_down = across_x(up[2]), across_x(down[2])
    pieces = [(packed, 0, 0), (crossed, 1, 0)]
    pieces += [(up[k], 0, -k) for k in range(1, 5)] + [(down[k], 0, k) for k in range(1, 4)]
    pieces += [(along_z(crossed, 1), 1, -1), (along_z(crossed, -1), 1, 1), (far_up, 1, -2), (far_down, 1, 2)]
    pieces += [(along_z(far_up, 1), 1, -3), (along_z(far_down, -1), 1, 3), (across_x(up[4]), 1, 4)]
    arrays = [p[0] for p in pieces] + [across_core(p[0]) for p in pieces]
    relative = [(s, dz, c) for c in range(2) for _, s, dz in pieces]
    (inputs, top, table, wqt, wot, gain_row, scale, probs, q, bdk, bdv,
     mine, other) = forward(
        relative, place, stashed, grad_top, tables(), arrays)
    fixed = (inputs, gain_row, scale, wqt, wot, probs, q, bdk, bdv, table)

    arriving = [top] * MB
    state = None
    for hop in range(LAYERS - 1):
        for m in range(MB):
            out, *state = tick(hop, m, place, fixed, arriving[m], state)
            arriving[m] = lax.ppermute(out, "section", [(LAYERS - 1 - hop, LAYERS - 2 - hop)])
        if hop == 0:
            mine, other, state[0] = lax.optimization_barrier((mine, other, state[0]))
            crossed_halves = across_x(other)
    own, across = [], []
    for m in range(MB):
        if m == 2:
            crossed_halves, state[0] = lax.optimization_barrier((crossed_halves, state[0]))
        *state, payload = tick(LAYERS - 1, m, place, fixed, arriving[m], state)
        if handed_on(m):
            own.append(payload)
            across.append(across_x(payload))
    *own_across, grads_in = lax.optimization_barrier((*own, *across, state[0]))
    payload = own_across + [across_core(v) for v in own_across]
    blocks = [mine, crossed_halves, across_core(mine), across_core(crossed_halves)]
    out_chunks = out_terms(place, blocks, payload)
    qkv_chunks, grads_in = qkv_terms(place, blocks, payload, grads_in)

    def added(a, b):
        return (a.astype(F32) + b.astype(F32)).astype(BF)

    def summed(chunks):
        half = chunks[4].shape[0] // 2
        up, down = along_z(chunks[4][:half], 1), along_z(chunks[4][half:], -1)
        up = jnp.concatenate([added(up, chunks[3][:half]), chunks[3][half:]], axis=0)
        down = jnp.concatenate([chunks[5][:half], added(down, chunks[5][half:])], axis=0)
        for k in (2, 1, 0):
            up, down = along_z(up, 1), along_z(down, -1)
            if k:
                up, down = added(up, chunks[k]), added(down, chunks[8 - k])
        return [chunks[0], up, down]

    out_parts = summed(out_chunks)
    kept_qkv, other_qkv, kept_out, other_out = add_terms(place, summed(qkv_chunks) + out_parts)
    qkv_grad, out_grad, gain_grad = finish(
        place, kept_qkv, across_core(other_qkv), kept_out, across_core(other_out), qkv_weight, norm_gain)
    return (grads_in.reshape(1, TOK, D), gain_grad, qkv_grad, out_grad)


def solution(mesh):
    in_specs = (
        P("section", "dp", None),
        P("dp", None),
        P("dp"),
        P("section", "dp"),
        P("section", "dp", None),
        P("section", "dp", None),
    )
    out_specs = (
        P("section", "dp", None),
        P("section", "dp"),
        P("section", "dp", None),
        P("section", "dp", None),
    )
    return jax.shard_map(body, mesh=mesh, in_specs=in_specs, out_specs=out_specs, check_vma=False)
```

```python
from functools import partial

import jax
import jax.numpy as jnp
import numpy as np
from jax import lax
from jax.experimental import pallas as pl
from jax.experimental.pallas import tpu as pltpu
from jax.sharding import PartitionSpec as P

D = 2048
HD = 64
SEQLEN = 32
QW = 1024
KVW = 128
QKVW = 1280
TOK = 128
MB = 4
NB = TOK // MB
LAYERS = 8
NZ = 8
NDP = 32
QUADS = 4
QL = 256
JL = 4 * NB
EPSILON = 1e-05
ROPE_BASE = 10000.0
BF = jnp.bfloat16
F32 = jnp.float32
VMEM_LIMIT = 28 << 20
SMALL_LIMIT = 12 << 20
SEC, XP, ZP, CORE = range(4)
PACKW = QKVW + 1024 + 128

ANY = pl.BlockSpec(memory_space=pl.ANY)
VM = pl.BlockSpec(memory_space=pltpu.VMEM)
SM = pl.BlockSpec(memory_space=pltpu.SMEM)


def held(value):
    return pltpu.with_memory_space_constraint(value, pltpu.VMEM)


def in_hbm(value):
    return pltpu.with_memory_space_constraint(value, pltpu.HBM)


def nn(a, b):
    return lax.dot_general(a, b, (((1,), (0,)), ((), ())), preferred_element_type=F32)


def nt(a, b):
    return lax.dot_general(a, b, (((1,), (1,)), ((), ())), preferred_element_type=F32)


def tn(a, b):
    return lax.dot_general(a, b, (((0,), (0,)), ((), ())), preferred_element_type=F32)


def rotate(u, cosine, sine):
    rows = u.shape[0]
    lane = lax.broadcasted_iota(jnp.int32, (rows, 128), 1)
    first = (lane & 63) < 32
    parts = []
    for i in range(u.shape[1] // 128):
        block = u[:, i * 128 : (i + 1) * 128]
        swapped = jnp.where(first, pltpu.roll(block, 96, 1), pltpu.roll(block, 32, 1))
        parts.append(block * cosine + swapped * sine)
    return parts[0] if len(parts) == 1 else jnp.concatenate(parts, axis=1)


def run_sums(values):
    rows = values.shape[0]
    run = lax.broadcasted_iota(jnp.int32, (rows, 128), 1) // NB
    parts = []
    for i in range(values.shape[1] // 128):
        block = values[:, i * 128 : (i + 1) * 128]
        out = jnp.zeros_like(block)
        for r in range(128 // NB):
            total = jnp.sum(jnp.where(run == r, block, 0.0), axis=1, keepdims=True)
            out = jnp.where(run == r, total, out)
        parts.append(out)
    return parts[0] if len(parts) == 1 else jnp.concatenate(parts, axis=1)


def block_diagonal_mask():
    row = lax.broadcasted_iota(jnp.int32, (JL, QL), 0)
    lane = lax.broadcasted_iota(jnp.int32, (JL, QL), 1)
    return (row // NB) == (lane >> 6)


def block_diagonal(rows128, group, mask):
    lane = lax.broadcasted_iota(jnp.int32, rows128.shape, 1)
    other = pltpu.roll(rows128, 64, 1)
    keep = (lane < 64) if group == 0 else (lane >= 64)
    twice = jnp.where(keep, rows128, other)
    wide = jnp.concatenate([twice, twice], axis=1)
    tall = jnp.concatenate([wide] * 4, axis=0)
    return jnp.where(mask, tall, 0.0).astype(BF)


def fold_diagonal(products, mask):
    kept = jnp.where(mask, products, 0.0)
    tall = kept[0:NB] + kept[NB : 2 * NB] + kept[2 * NB : 3 * NB] + kept[3 * NB :]
    pair = tall[:, :128] + tall[:, 128:]
    return pair + pltpu.roll(pair, 64, 1)


def pack_kernel(place, wq_ref, wo_ref, gain_ref, out_ref, gain_own, sems):
    copies = [
        pltpu.make_async_copy(gain_ref, gain_own, sems.at[0]),
        pltpu.make_async_copy(wq_ref.at[0], out_ref.at[:, pl.ds(0, QKVW)], sems.at[1]),
        pltpu.make_async_copy(
            wo_ref.at[0, :, pl.ds(0, 1024)], out_ref.at[pl.ds(0, 32), pl.ds(QKVW, 1024)], sems.at[2]),
        pltpu.make_async_copy(
            wo_ref.at[0, :, pl.ds(1024, 1024)], out_ref.at[pl.ds(32, 32), pl.ds(QKVW, 1024)], sems.at[3]),
    ]
    for copy in copies:
        copy.start()
    copies[0].wait()
    gain = gain_own[...].astype(F32)
    zero = jnp.zeros_like(gain)
    low = jnp.concatenate([gain, zero], axis=1)
    high = jnp.concatenate([zero, gain], axis=1)
    pair = jnp.where(place[CORE] == 0, low, high)
    out_ref[:, QKVW + 1024 :] = jnp.broadcast_to(pair, (64, 128)).astype(BF)
    for copy in copies[1:]:
        copy.wait()


def pack(place, wq, wo, gain):
    return pl.pallas_call(
        pack_kernel,
        out_shape=pltpu.VMEM((64, PACKW), BF),
        in_specs=[SM, ANY, ANY, ANY],
        out_specs=VM,
        scratch_shapes=[pltpu.VMEM((1, 64), BF), pltpu.SemaphoreType.DMA((4,))],
        compiler_params=pltpu.CompilerParams(vmem_limit_bytes=SMALL_LIMIT),
        name="pack",
    )(place, in_hbm(wq), in_hbm(wo), in_hbm(gain))


def forward_kernel(relative, place, x_hbm, top_hbm, table_hbm, *refs):
    pieces = refs[:32]
    (x_ref, top_ref, table_ref, wqt_ref, wot_ref, gain_ref, scale_ref, probs_ref, q_ref, bdk_ref, bdv_ref,
     mine_ref, other_ref,
     gain_pieces, wq_ref, wo_ref, sems) = refs[32:]
    copies = [
        pltpu.make_async_copy(source, target, sems.at[i])
        for i, (source, target) in enumerate(((x_hbm.at[0], x_ref), (table_hbm, table_ref), (top_hbm, top_ref)))
    ]
    for copy in copies:
        copy.start()
    for i, piece in enumerate(pieces):
        swap_x, step, swap_core = relative[i]
        owner = dp_index(place[XP] ^ swap_x, (place[ZP] + step) & 7, place[CORE] ^ swap_core)
        row64 = pl.multiple_of(owner * 64, 64)
        row32 = pl.multiple_of(owner * 32, 32)
        row16 = pl.multiple_of(owner * 16, 16)
        gain_pieces[pl.ds(row16, 16), :] = piece[0:16, QKVW + 1024 :]
        wq_ref[pl.ds(row64, 64), :] = piece[:, :QKVW]
        wo_ref[pl.ds(row32, 32), pl.ds(0, 1024)] = piece[0:32, QKVW : QKVW + 1024]
        wo_ref[pl.ds(row32, 32), pl.ds(1024, 1024)] = piece[32:64, QKVW : QKVW + 1024]
    copies[0].wait()
    wide = x_ref[...].astype(F32)
    inverse = lax.rsqrt(jnp.sum(wide * wide, axis=1, keepdims=True) * (1.0 / D) + EPSILON)
    scale_ref[...] = jnp.broadcast_to(inverse, (TOK, 128))
    mask = block_diagonal_mask()
    attended = {}
    for i in range(16):
        both = (gain_pieces[pl.ds(32 * i, 1), :].astype(F32)
                + gain_pieces[pl.ds(32 * i + 16, 1), :].astype(F32))
        gain_ref[:, pl.ds(128 * i, 128)] = jnp.broadcast_to(both, (8, 128))
    normed = (wide * inverse * gain_ref[0:1, :]).astype(BF)
    right = place[XP] == 1
    for i in range(NZ):
        low = normed[:, i * 128 : (i + 1) * 128]
        high = normed[:, 1024 + i * 128 : 1024 + (i + 1) * 128]
        mine_ref[i] = jnp.where(right, high, low)
        other_ref[i] = jnp.where(right, low, high)
    projected = nn(normed, wq_ref[...])
    for i in range(8):
        wqt_ref[:, i * 256 : (i + 1) * 256] = wq_ref[i * 256 : (i + 1) * 256, :].T
    for i in range(4):
        wot_ref[:, i * 256 : (i + 1) * 256] = wo_ref[i * 256 : (i + 1) * 256, :].T
    copies[1].wait()
    cosine = table_ref[:, :128]
    sine = table_ref[:, 128:]
    queries = rotate(projected[:, :QW], cosine, sine).astype(BF)
    keys = rotate(projected[:, QW : QW + KVW], cosine, sine).astype(BF).astype(F32)
    values = projected[:, QW + KVW :].astype(BF).astype(F32)
    row = lax.broadcasted_iota(jnp.int32, (NB, JL), 0)
    lane = lax.broadcasted_iota(jnp.int32, (NB, JL), 1) & (NB - 1)
    for m in range(MB):
        rows = slice(m * NB, (m + 1) * NB)
        allowed = (lane <= row) & (lane < place[4 + m])
        for g in range(2):
            bdk = block_diagonal(keys[rows], g, mask)
            bdv = block_diagonal(values[rows], g, mask)
            bdk_ref[m, g] = bdk
            bdv_ref[m, g] = bdv
            for t in (2 * g, 2 * g + 1):
                quad = queries[rows, t * QL : (t + 1) * QL]
                q_ref[m, pl.ds(t * NB, NB), :] = quad
                scores = nt(quad, bdk) * 0.125
                terms = jnp.where(allowed, jnp.exp(jnp.where(allowed, scores, 0.0)), 0.0)
                probs = terms / run_sums(terms)
                probs_ref[m, pl.ds(t * NB, NB), :] = probs
                got = nn(probs.astype(BF), bdv).astype(BF)
                attended[t] = got
        for i in range(2):
            low, high = attended[i], attended[2 + i]
            mine = jnp.where(right, high, low)
            other = jnp.where(right, low, high)
            for j in range(2):
                mine_ref[NZ + 2 * i + j, rows, :] = mine[:, j * 128 : (j + 1) * 128]
                other_ref[NZ + 2 * i + j, rows, :] = other[:, j * 128 : (j + 1) * 128]
    copies[2].wait()


def forward(relative, place, inputs, top, table, pieces):
    shapes = [
        ((TOK, D), BF), ((TOK, D), BF), ((TOK, 256), F32), ((QKVW, D), BF), ((D, QW), BF), ((8, D), F32),
        ((TOK, 128), F32), ((MB, QUADS * NB, JL), F32), ((MB, QUADS * NB, QL), BF),
        ((MB, 2, JL, QL), BF), ((MB, 2, JL, QL), BF),
        ((NZ + 4, TOK, 128), BF), ((NZ + 4, TOK, 128), BF),
    ]
    return pl.pallas_call(
        partial(forward_kernel, relative),
        out_shape=[pltpu.VMEM(s, t) for s, t in shapes],
        in_specs=[SM, ANY, ANY, ANY] + [VM] * 32,
        out_specs=[VM] * len(shapes),
        scratch_shapes=[
            pltpu.VMEM((NDP * 16, 128), BF), pltpu.VMEM((D, QKVW), BF), pltpu.VMEM((QW, D), BF),
            pltpu.SemaphoreType.DMA((3,))],
        compiler_params=pltpu.CompilerParams(vmem_limit_bytes=VMEM_LIMIT),
        name="forward",
    )(place, in_hbm(inputs), in_hbm(top), in_hbm(table), *[held(p) for p in pieces])


def handed_on(m):
    return {2: (0, 1, 2), 3: (3,)}.get(m, ())


def tick_kernel(hop, m, *refs):
    (place, x_ref, gain_ref, scale_ref, wqt_ref, wot_ref, probs_ref, q_ref, bdk_ref, bdv_ref,
     table_ref, cot_ref) = refs[:12]
    last = hop == LAYERS - 1
    if last:
        gi_ref, gp_ref, keep_ref, final_ref = refs[-4:]
    else:
        out_ref, gi_ref, gp_ref, keep_ref = refs[-4:]
    rows_m = slice(m * NB, (m + 1) * NB)

    @pl.when(place[SEC] == LAYERS - 1 - hop)
    def _():
        cot = cot_ref[rows_m, :] if hop == 0 else cot_ref[...]
        grad_att = nn(cot, wot_ref[...]).astype(BF)
        mask = block_diagonal_mask()
        cosine = table_ref[0:NB, :128]
        sine = -table_ref[0:NB, 128:]
        parts = []
        grad_keys = []
        grad_values = []
        for g in range(2):
            bdk = bdk_ref[m, g]
            bdv = bdv_ref[m, g]
            rows = pl.ds(g * 2 * NB, 2 * NB)
            quads = jnp.concatenate(
                [grad_att[:, (2 * g + i) * QL : (2 * g + i + 1) * QL] for i in range(2)], axis=0)
            probs = probs_ref[m, rows, :]
            grad_probs = nt(quads, bdv)
            centre = run_sums(probs * grad_probs)
            grad_scores = (probs * (grad_probs - centre) * 0.125).astype(BF)
            grad_q = nn(grad_scores, bdk)
            parts.append(grad_q[:NB])
            parts.append(grad_q[NB:])
            grad_keys.append(fold_diagonal(tn(grad_scores, q_ref[m, rows, :]), mask))
            grad_values.append(fold_diagonal(tn(probs.astype(BF), quads), mask))
        lane = lax.broadcasted_iota(jnp.int32, (NB, 128), 1)
        key_rows = jnp.where(lane < 64, grad_keys[0], grad_keys[1])
        value_rows = jnp.where(lane < 64, grad_values[0], grad_values[1])
        rotated = rotate(jnp.concatenate(parts + [key_rows], axis=1), cosine, sine)
        gp = jnp.concatenate([rotated, value_rows], axis=1).astype(BF)
        gp_ref[m] = gp
        keep_ref[m] = cot
        grad_hat = nn(gp, wqt_ref[...]) * gain_ref[0:1, :]
        wide = x_ref[rows_m, :].astype(F32)
        inverse = scale_ref[rows_m, 0:1]
        mean = jnp.sum(grad_hat * wide, axis=1, keepdims=True) * (1.0 / D)
        inner = inverse * (grad_hat - wide * (inverse * inverse * mean))
        grads = (cot.astype(F32) + inner).astype(BF)
        gi_ref[m] = grads
        if not last:
            out_ref[...] = grads

    if last:
        for i, source in enumerate(handed_on(m)):
            final_ref[i * NB : (i + 1) * NB, :QKVW] = gp_ref[source]
            final_ref[i * NB : (i + 1) * NB, QKVW:] = keep_ref[source]


def tick(hop, m, place, fixed, cot, state):
    args = [held(v) for v in fixed] + [cot if hop else held(cot)]
    last = hop == LAYERS - 1
    outs = [pltpu.VMEM((MB, NB, w), BF) for w in (D, QKVW, D)]
    if last:
        outs = outs + [pltpu.VMEM((max(1, len(handed_on(m))) * NB, QKVW + D), BF)]
    else:
        outs = [jax.ShapeDtypeStruct((NB, D), BF)] + outs
    aliases = {}
    for i, value in enumerate(state or []):
        aliases[1 + len(args)] = i if last else i + 1
        args.append(held(value))
    return pl.pallas_call(
        partial(tick_kernel, hop, m),
        out_shape=outs,
        in_specs=[SM] + [VM] * len(args),
        out_specs=[VM] * len(outs),
        input_output_aliases=aliases,
        compiler_params=pltpu.CompilerParams(vmem_limit_bytes=VMEM_LIMIT),
        name="tick",
    )(place, *args)


def columns(refs, core, width, start=0):
    first = pl.multiple_of(core * width, 128)
    return jnp.concatenate([r[:, pl.ds(first + start, width)] for r in refs], axis=0)


def qkv_terms_kernel(place, *refs):
    halves, payload = refs[:4], refs[4:12]
    grads, outs, grads_out, sem = refs[12], refs[13 : 13 + NZ], refs[-2], refs[-1]
    copy = pltpu.make_async_copy(grads, grads_out, sem.at[0])
    copy.start()
    right = columns(payload, place[CORE], 640)
    for k in range(NZ):
        chunk = (place[ZP] + k) & 7
        left = jnp.concatenate([r[chunk] for r in halves], axis=0)
        outs[k][...] = tn(left, right).astype(BF)
    copy.wait()


def out_terms_kernel(place, *refs):
    halves, payload = refs[:4], refs[4:12]
    outs, scratch = refs[12 : 12 + NZ], refs[-1]
    left = jnp.concatenate(
        [jnp.concatenate([r[NZ + j] for j in range(4)], axis=1) for r in halves], axis=0)
    total = tn(left, columns(payload, place[CORE], 1024, QKVW)).astype(BF)
    for z in range(NZ):
        scratch[z] = total[z * 64 : (z + 1) * 64]
    for k in range(NZ):
        outs[k][...] = scratch[(place[ZP] + k) & 7]


def qkv_terms(place, halves, payload, grads):
    *chunks, grads = pl.pallas_call(
        qkv_terms_kernel,
        out_shape=[jax.ShapeDtypeStruct((128, 640), BF)] * NZ + [pltpu.HBM((MB, NB, D), BF)],
        in_specs=[SM] + [VM] * 13,
        out_specs=[VM] * NZ + [ANY],
        scratch_shapes=[pltpu.SemaphoreType.DMA((1,))],
        compiler_params=pltpu.CompilerParams(vmem_limit_bytes=VMEM_LIMIT),
        name="qkv_terms",
    )(place, *halves, *payload, held(grads))
    return chunks, grads


def out_terms(place, halves, payload):
    return pl.pallas_call(
        out_terms_kernel,
        out_shape=[jax.ShapeDtypeStruct((64, 1024), BF)] * NZ,
        in_specs=[SM] + [VM] * 12,
        out_specs=[VM] * NZ,
        scratch_shapes=[pltpu.VMEM((NZ, 64, 1024), BF)],
        compiler_params=pltpu.CompilerParams(vmem_limit_bytes=VMEM_LIMIT),
        name="out_terms",
    )(place, *halves, *payload)


def add_kernel(place, *refs):
    first = place[CORE] == 0
    for i in range(2):
        own, up, down = refs[3 * i : 3 * i + 3]
        kept, other = refs[6 + 2 * i : 8 + 2 * i]
        total = own[...].astype(F32) + up[...].astype(F32) + down[...].astype(F32)
        half = total.shape[0] // 2
        kept[...] = jnp.where(first, total[:half], total[half:])
        other[...] = jnp.where(first, total[half:], total[:half])


def add_terms(place, parts):
    shapes = [(v.shape[0] // 2, v.shape[1]) for v in (parts[0], parts[0], parts[3], parts[3])]
    return pl.pallas_call(
        add_kernel,
        out_shape=[jax.ShapeDtypeStruct(s, F32) for s in shapes],
        in_specs=[SM] + [VM] * len(parts),
        out_specs=[VM] * len(shapes),
        compiler_params=pltpu.CompilerParams(vmem_limit_bytes=SMALL_LIMIT),
        name="add_terms",
    )(place, *parts)


def join(place, kept, other):
    first = place[CORE] == 0
    left = jnp.where(first, kept[...], other[...])
    right = jnp.where(first, other[...], kept[...])
    return jnp.concatenate([left, right], axis=1)


def finish_kernel(place, kept_qkv, other_qkv, kept_out, other_out, wq_ref, gain_ref, qkv_ref, out_ref, gain_out):
    out_ref[0] = join(place, kept_out, other_out)
    total = join(place, kept_qkv, other_qkv)
    qkv_ref[0] = total
    column = jnp.sum(total * wq_ref[0].astype(F32), axis=1, keepdims=True)
    row = lax.broadcasted_iota(jnp.int32, (64, 64), 0)
    lane = lax.broadcasted_iota(jnp.int32, (64, 64), 1)
    sums = jnp.sum(jnp.where(row == lane, column, 0.0), axis=0, keepdims=True)
    gain_out[...] = sums / gain_ref[...].astype(F32)


def finish(place, *args):
    shapes = [(1, 64, QKVW), (1, 32, D), (1, 64)]
    return pl.pallas_call(
        finish_kernel,
        out_shape=[jax.ShapeDtypeStruct(s, F32) for s in shapes],
        in_specs=[SM] + [VM] * len(args),
        out_specs=[VM] * len(shapes),
        compiler_params=pltpu.CompilerParams(vmem_limit_bytes=SMALL_LIMIT),
        name="finish",
    )(place, *args)


def tables():
    half = HD // 2
    inverse_freq = ROPE_BASE ** (-(np.arange(half) * 2.0 / HD))
    angles = np.arange(SEQLEN)[:, None] * inverse_freq[None, :]
    sine = np.sin(angles)
    cosine = np.tile(np.cos(angles), (TOK // SEQLEN, 4))
    sine = np.tile(np.concatenate([-sine, sine], axis=1), (TOK // SEQLEN, 2))
    return jnp.asarray(np.concatenate([cosine, sine], axis=1), F32)


def dp_index(x, z, c):
    return (x * NZ + z) * 2 + c


def along_z(value, steps):
    return lax.ppermute(value, "dp", [
        (dp_index(x, z, c), dp_index(x, (z + steps) % NZ, c))
        for x in range(2) for z in range(NZ) for c in range(2)])


def across_x(value):
    return lax.ppermute(value, "dp", [(i, i ^ 16) for i in range(NDP)])


def across_core(value):
    return lax.ppermute(value, "dp", [(i, i ^ 1) for i in range(NDP)])


def body(stashed, grad_top, lengths, norm_gain, qkv_weight, out_weight):
    dp = lax.axis_index("dp")
    place = jnp.stack([lax.axis_index("section"), dp // 16, (dp // 2) % NZ, dp % 2]).astype(jnp.int32)
    place = jnp.concatenate([place, lengths])

    packed = pack(place, qkv_weight, out_weight, norm_gain)
    crossed = across_x(packed)
    up, down = [packed], [packed]
    for k in range(1, 5):
        up.append(along_z(up[-1], 1))
    for k in range(1, 4):
        down.append(along_z(down[-1], -1))
    far_up, far_down = across_x(up[2]), across_x(down[2])
    pieces = [(packed, 0, 0), (crossed, 1, 0)]
    pieces += [(up[k], 0, -k) for k in range(1, 5)] + [(down[k], 0, k) for k in range(1, 4)]
    pieces += [(along_z(crossed, 1), 1, -1), (along_z(crossed, -1), 1, 1), (far_up, 1, -2), (far_down, 1, 2)]
    pieces += [(along_z(far_up, 1), 1, -3), (along_z(far_down, -1), 1, 3), (across_x(up[4]), 1, 4)]
    arrays = [p[0] for p in pieces] + [across_core(p[0]) for p in pieces]
    relative = [(s, dz, c) for c in range(2) for _, s, dz in pieces]
    (inputs, top, table, wqt, wot, gain_row, scale, probs, q, bdk, bdv,
     mine, other) = forward(
        relative, place, stashed, grad_top, tables(), arrays)
    fixed = (inputs, gain_row, scale, wqt, wot, probs, q, bdk, bdv, table)

    arriving = [top] * MB
    state = None
    for hop in range(LAYERS - 1):
        for m in range(MB):
            out, *state = tick(hop, m, place, fixed, arriving[m], state)
            top_of_two = LAYERS - 1 - hop // 2 * 2
            pairs = [(p, p - 1) for p in (top_of_two, top_of_two - 1) if p > 0]
            arriving[m] = lax.ppermute(out, "section", pairs)
        if hop == 0:
            mine, other, state[0] = lax.optimization_barrier((mine, other, state[0]))
            crossed_halves = across_x(other)
    own, across = [], []
    for m in range(MB):
        if m == 2:
            crossed_halves, state[0] = lax.optimization_barrier((crossed_halves, state[0]))
        *state, payload = tick(LAYERS - 1, m, place, fixed, arriving[m], state)
        if handed_on(m):
            own.append(payload)
            across.append(across_x(payload))
    *own_across, grads_in = lax.optimization_barrier((*own, *across, state[0]))
    payload = own_across + [across_core(v) for v in own_across]
    blocks = [mine, crossed_halves, across_core(mine), across_core(crossed_halves)]
    out_chunks = out_terms(place, blocks, payload)
    qkv_chunks, grads_in = qkv_terms(place, blocks, payload, grads_in)

    def added(a, b):
        return (a.astype(F32) + b.astype(F32)).astype(BF)

    def summed(chunks):
        half = chunks[4].shape[0] // 2
        up, down = along_z(chunks[4][:half], 1), along_z(chunks[4][half:], -1)
        up = jnp.concatenate([added(up, chunks[3][:half]), chunks[3][half:]], axis=0)
        down = jnp.concatenate([chunks[5][:half], added(down, chunks[5][half:])], axis=0)
        for k in (2, 1, 0):
            up, down = along_z(up, 1), along_z(down, -1)
            if k:
                up, down = added(up, chunks[k]), added(down, chunks[8 - k])
        return [chunks[0], up, down]

    out_parts = summed(out_chunks)
    kept_qkv, other_qkv, kept_out, other_out = add_terms(place, summed(qkv_chunks) + out_parts)
    qkv_grad, out_grad, gain_grad = finish(
        place, kept_qkv, across_core(other_qkv), kept_out, across_core(other_out), qkv_weight, norm_gain)
    return (grads_in.reshape(1, TOK, D), gain_grad, qkv_grad, out_grad)


def solution(mesh):
    in_specs = (
        P("section", "dp", None),
        P("dp", None),
        P("dp"),
        P("section", "dp"),
        P("section", "dp", None),
        P("section", "dp", None),
    )
    out_specs = (
        P("section", "dp", None),
        P("section", "dp"),
        P("section", "dp", None),
        P("section", "dp", None),
    )
    return jax.shard_map(body, mesh=mesh, in_specs=in_specs, out_specs=out_specs, check_vma=False)
```
